128 devices in a mesh: section: 16 (over z_lo, x, core), tp: 8 (over y, z_hi).
Axes of the slice: x: 4, y: 4, z: 4 (z_hi: 2, z_lo: 2; z = z_hi * 2 + z_lo), core: 2. Of those that a mesh axis runs over, the one named last changes fastest.
Arguments:
- tokens: bfloat16 [16, 256, 4096], P('section', None, 'tp'), may hold values from -96 to 96
- cotangent: bfloat16 [16, 256, 4096], P('section', None, 'tp'), may hold values from -6 to 6
- memory: bfloat16 [1024, 4096], P('section', 'tp'), may hold values from -12 to 12
- w_query: bfloat16 [16, 4096, 4096], P('section', None, 'tp'), may hold values from -0.1875 to 0.1875
- w_key: bfloat16 [16, 4096, 4096], P('section', None, 'tp'), may hold values from -0.1875 to 0.1875
- w_value: bfloat16 [16, 4096, 4096], P('section', None, 'tp'), may hold values from -0.09375 to 0.09375
- w_out: bfloat16 [16, 4096, 4096], P('section', 'tp'), may hold values from -0.09375 to 0.09375
Outputs:
- attended_out: bfloat16 [16, 256, 4096], P('section', None, 'tp')
- grad_tokens: bfloat16 [16, 256, 4096], P('section', None, 'tp')
- grad_memory: bfloat16 [1024, 4096], P('section', 'tp')
The draws below stay inside these ranges and needn't reach their ends.
All inputs are finite; a program needn't handle non-finite values.
Results may differ from the reference program's by a relative error of at most 0.02.
Values may be sent and summed in bfloat16 or wider, within the bound.
A program may use at most 128 MiB of HBM per device.

```python
import jax
import jax.numpy as jnp
from jax import lax

D = 4096
ATTENTION_HEADS = 16
HEAD_SIZE = 256
MEMORY_TOKENS = 1024
TARGET_TOKENS = 256
LAYERS = 16
INNER = 4096


def memory_rows(key):
    base = jnp.clip(jax.random.normal(jax.random.fold_in(key, 101), (MEMORY_TOKENS, D), jnp.float32), -6.0, 6.0)
    position = jnp.arange(MEMORY_TOKENS)[:, None]
    paired = (position >= MEMORY_TOKENS - 8) & (position % 2 == 1)
    return jnp.where(paired, base, base)


def weight_pair(key):
    first = jnp.clip(jax.random.normal(jax.random.fold_in(key, 201), (LAYERS, D, INNER), jnp.float32), -6.0, 6.0)
    second = jnp.clip(jax.random.normal(jax.random.fold_in(key, 202), (LAYERS, D, INNER), jnp.float32), -6.0, 6.0)
    norm_factor = D ** (-0.5)
    return (norm_factor * first, norm_factor * second)


def draw_memory(key, part):
    rows = memory_rows(key)
    return rows.astype(jnp.bfloat16)


def draw_tokens(key, part):
    key = jax.random.fold_in(key, 11)
    values = jnp.clip(jax.random.normal(key, (LAYERS, TARGET_TOKENS, D), jnp.float32), -6.0, 6.0)
    return values.astype(jnp.bfloat16)


def draw_w_query(key, part):
    first, second = weight_pair(key)
    return first.astype(jnp.bfloat16)


def draw_w_key(key, part):
    first, second = weight_pair(key)
    return second.astype(jnp.bfloat16)


def block_scale(key, shape, split, least, top_value):
    def one(dim, shards_of):
        heights = jax.random.uniform(jax.random.fold_in(jax.random.fold_in(key, 6), dim), (shards_of,), jnp.float32, least / len(split), top_value / len(split))
        return jnp.repeat(jnp.exp(heights), shape[dim] // shards_of).reshape((-1,) + (1,) * (len(shape) - dim - 1))

    factor_of = one(*split[0])
    for cut in split[1:]:
        factor_of = factor_of * one(*cut)
    return factor_of


def noise(rng, extent, scale, limit, shards=(), dtype=jnp.bfloat16):
    result = scale * jax.random.normal(rng, extent, jnp.float32)
    if shards:
        result = result * block_scale(rng, extent, shards, -0.22, 0.18)
    return jnp.clip(result, -limit, limit).astype(dtype)


def setup_inputs(seed: int = 0) -> dict:
    streams_of = jax.random.split(jax.random.key(seed), 8)
    tokens = draw_tokens(jax.random.fold_in(streams_of[7], 71), 0)
    cotangent = noise(streams_of[1], (LAYERS, TARGET_TOKENS, D), 1.0, 6.0, ((0, 16), (2, 8)))
    memory = draw_memory(jax.random.fold_in(streams_of[7], 71), 0)
    w_query = draw_w_query(jax.random.fold_in(streams_of[7], 71), 0)
    w_key = draw_w_key(jax.random.fold_in(streams_of[7], 71), 0)
    w_value = noise(streams_of[5], (LAYERS, D, INNER), D ** -0.5, 0.09375, ((0, 16), (2, 8)))
    w_out = noise(streams_of[6], (LAYERS, INNER, D), INNER ** -0.5, 0.09375, ((0, 16), (1, 8)))
    return dict(tokens=tokens, cotangent=cotangent, memory=memory, w_query=w_query, w_key=w_key, w_value=w_value, w_out=w_out)


def section_pass(target, grad_out, memory, w_query, w_key, w_value, w_out):
    score_scale = HEAD_SIZE ** -0.5
    queries = jnp.dot(target, w_query, preferred_element_type=jnp.float32).astype(jnp.bfloat16)
    keys = jnp.dot(memory, w_key, preferred_element_type=jnp.float32).astype(jnp.bfloat16)
    values = jnp.dot(memory, w_value, preferred_element_type=jnp.float32).astype(jnp.bfloat16)
    query_per_head = queries.reshape(TARGET_TOKENS, ATTENTION_HEADS, HEAD_SIZE).astype(jnp.float32)
    key_per_head = keys.reshape(MEMORY_TOKENS, ATTENTION_HEADS, HEAD_SIZE).astype(jnp.float32)
    value_per_head = values.reshape(MEMORY_TOKENS, ATTENTION_HEADS, HEAD_SIZE).astype(jnp.float32)
    attention_scores = jnp.einsum("iws,jws->wij", query_per_head, key_per_head) * score_scale
    top = jnp.max(attention_scores, axis=-1, keepdims=True)
    weights = jnp.exp(attention_scores - top)
    probs = weights / jnp.sum(weights, axis=-1, keepdims=True)
    probabilities_batch = probs.astype(jnp.bfloat16).astype(jnp.float32)
    context_output = jnp.einsum("crb,bcl->rcl", probabilities_batch, value_per_head).astype(jnp.bfloat16).reshape(TARGET_TOKENS, ATTENTION_HEADS * HEAD_SIZE)
    attended = jnp.dot(context_output, w_out, preferred_element_type=jnp.float32).astype(jnp.bfloat16)
    grad_context = jnp.dot(grad_out, w_out.T, preferred_element_type=jnp.float32).astype(jnp.bfloat16)
    gradient_heads = grad_context.reshape(TARGET_TOKENS, ATTENTION_HEADS, HEAD_SIZE).astype(jnp.float32)
    probability_gradient = jnp.einsum("iws,jws->wij", gradient_heads, value_per_head)
    delta = jnp.sum(probability_gradient * probs, axis=-1, keepdims=True)
    value_gradient = jnp.einsum("cry,rcs->ycs", probabilities_batch, gradient_heads).astype(jnp.bfloat16).reshape(MEMORY_TOKENS, ATTENTION_HEADS * HEAD_SIZE)
    score_gradient = (probs * (probability_gradient - delta) * score_scale).astype(jnp.bfloat16).astype(jnp.float32)
    query_gradient = jnp.einsum("crb,bcl->rcl", score_gradient, key_per_head).astype(jnp.bfloat16).reshape(TARGET_TOKENS, ATTENTION_HEADS * HEAD_SIZE)
    key_gradient = jnp.einsum("cry,rcs->ycs", score_gradient, query_per_head).astype(jnp.bfloat16).reshape(MEMORY_TOKENS, ATTENTION_HEADS * HEAD_SIZE)
    grad_target = jnp.dot(query_gradient, w_query.T, preferred_element_type=jnp.float32).astype(jnp.bfloat16)
    grad_mem = jnp.dot(key_gradient, w_key.T, preferred_element_type=jnp.float32)
    grad_mem = grad_mem + jnp.dot(value_gradient, w_value.T, preferred_element_type=jnp.float32)
    return attended, grad_target, grad_mem


def reference(tokens, cotangent, memory, w_query, w_key, w_value, w_out):
    def step(total, layer):
        target, grad_out, wq_layer, wk_layer, wv_layer, wo_layer = layer
        attended, grad_target, grad_mem = section_pass(target, grad_out, memory, wq_layer, wk_layer, wv_layer, wo_layer)
        return total + grad_mem, (attended, grad_target)

    start = jnp.zeros((MEMORY_TOKENS, D), jnp.float32)
    total, stacked = lax.scan(step, start, (tokens, cotangent, w_query, w_key, w_value, w_out))
    return stacked[0], stacked[1], total.astype(jnp.bfloat16)
```

```python
import functools

import jax
import jax.numpy as jnp
from jax import lax
from jax.experimental import pallas as pl
from jax.experimental.pallas import tpu as pltpu
from jax.sharding import PartitionSpec as P

HEAD_SIZE = 256
HEADS = 2
FEATURES = 512
D = 4096
TARGETS = 256
MEMORY = 1024
OWN_ROWS = 64
SIDE = 2048
SCALE = HEAD_SIZE ** -0.5
BF16 = jnp.bfloat16
F32 = jnp.float32
N_SEMS = 128
N_LOCAL = 48


def dot(a, b):
    return lax.dot_general(a, b, (((1,), (0,)), ((), ())), preferred_element_type=F32)


def dot_nt(a, b):
    return lax.dot_general(a, b, (((1,), (1,)), ((), ())), preferred_element_type=F32)


def dot_tn(a, b):
    return lax.dot_general(a, b, (((0,), (0,)), ((), ())), preferred_element_type=F32)


def aligned(start, size):
    return pl.ds(pl.multiple_of(start, size), size)


def add_rows(dst, srcs):
    rows = dst.shape[0]

    def step(i, _):
        part = aligned(i * 16, 16)
        total = srcs[0][part, :].astype(F32)
        for src in srcs[1:]:
            total = total + src[part, :].astype(F32)
        dst[part, :] = total.astype(dst.dtype)
        return 0

    lax.fori_loop(0, rows // 16, step, 0)


def kernel(
    tokens, cotangent, memory, w_query, w_key, w_value, w_out,
    attended, grad_tokens, grad_memory,
    wkv, wq, wo, mem, tok, cot, kv, gkv, queries, gctx, ctx, gq, probs, probs_b, dscores,
    core_in, relay_in, final_in, z_in, y_in, att_in, att_z, tgt_in, tgt_z,
    send_sem, recv_sem, local_sem,
):
    section = lax.axis_index("section")
    tp = lax.axis_index("tp")
    c = lax.rem(section, 2)
    x = lax.rem(section // 2, 4)
    y = tp // 2
    zh = lax.rem(tp, 2)
    z = zh * 2 + section // 8

    def device(dx=0, dy=0, dz=0, dc=0):
        to_x, to_y, to_z = lax.rem(x + dx, 4), lax.rem(y + dy, 4), lax.rem(z + dz, 4)
        to_c = lax.rem(c + dc, 2)
        return ((lax.rem(to_z, 2) * 4 + to_x) * 2 + to_c, to_y * 2 + to_z // 2)

    counter = [0, 0]
    sends = []

    def remote(src, dst, where):
        i = counter[0]
        counter[0] += 1
        copy = pltpu.make_async_remote_copy(
            src_ref=src, dst_ref=dst, send_sem=send_sem.at[i], recv_sem=recv_sem.at[i],
            device_id=device(**where), device_id_type=pl.DeviceIdType.MESH,
        )
        copy.start()
        sends.append(copy)
        return copy

    def local(src, dst):
        i = counter[1]
        counter[1] += 1
        copy = pltpu.make_async_copy(src, dst, local_sem.at[i])
        copy.start()
        return copy

    def flush():
        for copy in sends:
            copy.wait_send()
        sends.clear()

    XP, XM, YP, YM = dict(dx=1), dict(dx=3), dict(dy=1), dict(dy=3)
    CORE, ZFAR = dict(dc=1), dict(dz=2)

    def x_at(dx):
        return lax.rem(x + dx, 4)

    def side(high):
        return aligned(high * SIDE, SIDE)

    def piece(dx, core, dz, half=None):
        to_z = lax.rem(z + dz, 4)
        row = core * 128 + lax.rem(to_z, 2) * 64
        rows = aligned(row, 64) if half is None else aligned(row + half * 32, 32)
        return mem.at[x_at(dx), rows, side(to_z // 2)]

    def block(buf, high, dy):
        return buf.at[:, aligned(high * SIDE + lax.rem(y + dy, 4) * FEATURES, FEATURES)]

    own_mem = mem.at[x, aligned(c * 128 + lax.rem(z, 2) * 64, 64), aligned(zh * SIDE + y * FEATURES, FEATURES)]
    near, far = zh, 1 - zh

    mem_load = local(memory, own_mem)
    tok_load = local(tokens.at[0], block(tok, near, 0))
    cot_load = local(cotangent.at[0], block(cot, near, 0))
    kv_loads, q_loads, o_loads = [], [], []
    for high in range(2):
        for row in range(4):
            src = pl.ds((row * 2 + high) * FEATURES, FEATURES)
            dst = pl.ds(high * SIDE + row * FEATURES, FEATURES)
            kv_loads.append(local(w_key.at[0, src, :], wkv.at[dst, pl.ds(0, FEATURES)]))
            kv_loads.append(local(w_value.at[0, src, :], wkv.at[dst, pl.ds(FEATURES, FEATURES)]))
    for high in range(2):
        for row in range(4):
            src = pl.ds((row * 2 + high) * FEATURES, FEATURES)
            dst = pl.ds(high * SIDE + row * FEATURES, FEATURES)
            q_loads.append(local(w_query.at[0, src, :], wq.at[dst, :]))
            o_loads.append(local(w_out.at[0, :, src], wo.at[:, dst]))

    barrier = pltpu.get_barrier_semaphore()
    peers = [XP, XM, YP, YM, dict(dy=2), dict(dz=1), dict(dz=3), ZFAR, CORE]
    for where in peers:
        pl.semaphore_signal(barrier, inc=1, device_id=device(**where), device_id_type=pl.DeviceIdType.MESH)
    pl.semaphore_wait(barrier, len(peers))

    mem_y = [remote(memory, own_mem, dict(dy=dy)) for dy in (1, 3, 2)]
    mem_load.wait()
    for copy in mem_y:
        copy.wait_recv()
    own = piece(0, c, 0)
    right, left, core_own = {}, {}, {}
    mem_z = {}

    def spread(dz):
        right[dz] = remote(piece(0, c, dz), piece(0, c, dz), XP)
        left[dz] = remote(piece(0, c, dz), piece(0, c, dz), XM)
        core_own[dz] = remote(piece(0, c, dz), piece(0, c, dz), CORE)

    right[0] = remote(own, own, XP)
    left[0] = remote(own, own, XM)
    for dz in (1, 3, 2):
        mem_z[dz] = remote(own, own, dict(dz=dz))
    core_own[0] = remote(own, own, CORE)

    def spread_targets(high, from_hbm):
        t = tokens.at[0] if from_hbm else block(tok, high, 0)
        g = cotangent.at[0] if from_hbm else block(cot, high, 0)
        t_dst, g_dst = block(tok, high, 0), block(cot, high, 0)
        t_right = remote(t, t_dst, YP)
        g_left = remote(g, g_dst, YM)
        g_right = remote(g, g_dst, YP)
        t_left = remote(t, t_dst, YM)
        return t_right, g_left, g_right, t_left

    near_ring = spread_targets(near, True)
    core_right, core_left, core_opposite = {}, {}, {}
    on_right, on_left = {}, {}

    def arrive_x(dz):
        right[dz].wait_recv()
        on_right[dz] = remote(piece(3, c, dz, 0), piece(3, c, dz, 0), XP)
        core_left[dz] = remote(piece(3, c, dz), piece(3, c, dz), CORE)
        left[dz].wait_recv()
        on_left[dz] = remote(piece(1, c, dz, 1), piece(1, c, dz, 1), XM)
        core_right[dz] = remote(piece(1, c, dz), piece(1, c, dz), CORE)

    def forward_targets(high, ring):
        t_right, g_left, g_right, t_left = ring
        t_right.wait_recv()
        t_on = remote(block(tok, high, 3), block(tok, high, 3), YP)
        g_left.wait_recv()
        g_on = remote(block(cot, high, 1), block(cot, high, 1), YM)
        return t_on, g_on

    def keys_values(dx):
        to_x = x_at(dx)
        rows = aligned(to_x * 256, 256)

        def step(n, _):
            cols = aligned(n * 256, 256)
            kv[rows, cols] = dot(mem[to_x], wkv[:, cols]).astype(BF16)
            return 0

        lax.fori_loop(0, 4, step, 0)

    arrive_x(0)
    for dz in (1, 3, 2):
        mem_z[4 - dz].wait_recv()
        spread(dz)
    tok_z = remote(tokens.at[0], block(tok, near, 0), ZFAR)
    cot_z = remote(cotangent.at[0], block(cot, near, 0), ZFAR)
    near_on = forward_targets(near, near_ring)
    for copy in kv_loads:
        copy.wait()
    for dz in (0, 1, 3, 2):
        core_own[dz].wait_recv()
    keys_values(0)
    arrive_x(1)
    arrive_x(3)
    tok_z.wait_recv()
    cot_z.wait_recv()
    far_ring = spread_targets(far, False)
    arrive_x(2)
    far_on = forward_targets(far, far_ring)

    def arrive_opposite(dz):
        on_right[dz].wait_recv()
        a = remote(piece(2, c, dz, 0), piece(2, c, dz, 0), CORE)
        on_left[dz].wait_recv()
        b = remote(piece(2, c, dz, 1), piece(2, c, dz, 1), CORE)
        core_opposite[dz] = (a, b)

    for dz in (0, 1):
        arrive_opposite(dz)
    for dz in (0, 1, 3, 2):
        core_right[dz].wait_recv()
    keys_values(1)
    for dz in (0, 1, 3, 2):
        core_left[dz].wait_recv()
    keys_values(3)
    for dz in (3, 2):
        arrive_opposite(dz)

    for ring, on in ((near_ring, near_on), (far_ring, far_on)):
        t_right, g_left, g_right, t_left = ring
        g_right.wait_recv()
        t_left.wait_recv()
        on[0].wait_recv()
        on[1].wait_recv()
    tok_load.wait()
    cot_load.wait()
    for copy in q_loads:
        copy.wait()
    for copy in o_loads:
        copy.wait()

    def project(n, _):
        cols = aligned(n * 256, 256)
        queries[:, cols] = dot(tok[...], wq[:, cols]).astype(BF16)
        gctx[:, cols] = dot_nt(cot[...], wo[cols, :]).astype(BF16)
        return 0

    lax.fori_loop(0, 2, project, 0)
    for dz in (0, 1, 3, 2):
        for copy in core_opposite[dz]:
            copy.wait_recv()
    keys_values(2)
    flush()

    for h in range(HEADS):
        k_cols = pl.ds(h * HEAD_SIZE, HEAD_SIZE)
        v_cols = pl.ds(FEATURES + h * HEAD_SIZE, HEAD_SIZE)
        scores = dot_nt(queries[:, k_cols], kv[:, k_cols]) * SCALE
        top = jnp.max(scores, axis=-1, keepdims=True)
        weights = jnp.exp(scores - top)
        p = weights / jnp.sum(weights, axis=-1, keepdims=True)
        probs[...] = p
        p_b = p.astype(BF16)
        probs_b[h] = p_b
        grad_probs = dot_nt(gctx[:, k_cols], kv[:, v_cols])
        p = probs[...]
        delta = jnp.sum(grad_probs * p, axis=-1, keepdims=True)
        ds = (p * (grad_probs - delta) * SCALE).astype(BF16)
        dscores[h] = ds
        gkv[:, k_cols] = dot_tn(ds, queries[:, k_cols]).astype(BF16)
        gkv[:, v_cols] = dot_tn(probs_b[h], gctx[:, k_cols]).astype(BF16)

    def memory_terms(dx):
        to_x = x_at(dx)
        rows = aligned(to_x * 256, 256)

        def step(n, _):
            cols = aligned(n * 512, 512)
            mem[to_x, :, cols] = dot_nt(gkv[rows, :], wkv[cols, :]).astype(BF16)
            return 0

        lax.fori_loop(0, 8, step, 0)
        return remote(mem.at[to_x, aligned((1 - c) * 128, 128), :], core_in.at[to_x], CORE)

    def core_piece(dx, dz):
        to_z = lax.rem(z + dz, 4)
        return core_in.at[x_at(dx), aligned(lax.rem(to_z, 2) * 64, 64), side(to_z // 2)]

    def pair_sum(dx, dz, extra=()):
        here = piece(dx, c, dz)
        add_rows(here, [here, core_piece(dx, dz)] + list(extra))
        return here

    GROUP_A, GROUP_B = (2, 3), (1, 0)
    core_2 = memory_terms(2)
    core_1 = memory_terms(1)
    core_2.wait_recv()
    relay_right, relay_left = {}, {}
    for i in range(2):
        relay_right[i] = remote(pair_sum(2, GROUP_A[i]), relay_in.at[0, i], XP)
        relay_left[i] = remote(pair_sum(2, GROUP_B[i]), relay_in.at[1, i], XM)
    core_3 = memory_terms(3)
    core_1.wait_recv()
    to_right, to_left = {}, {}
    for dz in GROUP_B:
        to_right[dz] = remote(pair_sum(1, dz), final_in.at[0, dz], XP)
    core_3.wait_recv()
    for dz in GROUP_A:
        to_left[dz] = remote(pair_sum(3, dz), final_in.at[1, dz], XM)
    core_0 = memory_terms(0)

    def ring_sum(buf, inbox, terms):
        terms(far, 2)
        a_relay = remote(block(buf, far, 2), inbox.at[0], YP)
        terms(near, 2)
        b_relay = remote(block(buf, near, 2), inbox.at[1], YM)
        terms(near, 1)
        b_right = remote(block(buf, near, 1), inbox.at[2], YP)
        terms(far, 3)
        a_left = remote(block(buf, far, 3), inbox.at[3], YM)
        terms(far, 1)
        terms(near, 3)
        terms(far, 0)
        terms(near, 0)
        return a_relay, b_relay, b_right, a_left

    def ring_relay(buf, inbox, copies):
        a_relay, b_relay, b_right, a_left = copies
        a_relay.wait_recv()
        here = block(buf, far, 1)
        add_rows(here, [here, inbox.at[0]])
        a_right = remote(here, inbox.at[4], YP)
        b_relay.wait_recv()
        here = block(buf, near, 3)
        add_rows(here, [here, inbox.at[1]])
        b_left = remote(here, inbox.at[5], YM)
        return b_right, a_left, a_right, b_left

    def ring_far(buf, inbox, z_box, copies):
        b_right, a_left, a_right, b_left = copies
        a_left.wait_recv()
        a_right.wait_recv()
        here = block(buf, far, 0)
        add_rows(here, [here, inbox.at[3], inbox.at[4]])
        return remote(here, z_box, ZFAR)

    def ring_near(buf, inbox, z_box, copies, z_copy, out):
        b_right, a_left, a_right, b_left = copies
        b_right.wait_recv()
        b_left.wait_recv()
        z_copy.wait_recv()
        add_rows(out.at[0], [block(buf, near, 0), inbox.at[2], inbox.at[5], z_box])

    for h in range(HEADS):
        cols = pl.ds(h * HEAD_SIZE, HEAD_SIZE)
        v_cols = pl.ds(FEATURES + h * HEAD_SIZE, HEAD_SIZE)
        ctx[:, cols] = dot(probs_b[h], kv[:, v_cols]).astype(BF16)

    def out_terms(high, dy):
        cols = aligned(high * SIDE + lax.rem(y + dy, 4) * FEATURES, FEATURES)
        tok[:, cols] = dot(ctx[...], wo[:, cols]).astype(BF16)

    att = ring_sum(tok, att_in, out_terms)

    for h in range(HEADS):
        cols = pl.ds(h * HEAD_SIZE, HEAD_SIZE)
        gq[:, cols] = dot(dscores[h], kv[:, cols]).astype(BF16)

    def target_terms(high, dy):
        rows = aligned(high * SIDE + lax.rem(y + dy, 4) * FEATURES, FEATURES)
        cot[:, rows] = dot_nt(gq[...], wq[rows, :]).astype(BF16)

    def x_relay(i):
        relay_right[i].wait_recv()
        dz = GROUP_A[i]
        to_right[dz] = remote(pair_sum(1, dz, [relay_in.at[0, i]]), final_in.at[0, dz], XP)
        relay_left[i].wait_recv()
        dz = GROUP_B[i]
        to_left[dz] = remote(pair_sum(3, dz, [relay_in.at[1, i]]), final_in.at[1, dz], XM)

    x_relay(0)
    att = ring_relay(tok, att_in, att)
    x_relay(1)
    tgt = ring_sum(cot, tgt_in, target_terms)
    core_0.wait_recv()
    att_far = ring_far(tok, att_in, att_z, att)
    tgt = ring_relay(cot, tgt_in, tgt)

    z_copies = {}

    def x_final(dz):
        to_right[dz].wait_recv()
        to_left[dz].wait_recv()
        here = pair_sum(0, dz, [final_in.at[0, dz], final_in.at[1, dz]])
        if dz:
            z_copies[dz] = remote(here, z_in.at[dz - 1], dict(dz=dz))

    x_final(2)
    x_final(1)
    ring_near(tok, att_in, att_z, att, att_far, attended)
    x_final(3)
    x_final(0)
    tgt_far = ring_far(cot, tgt_in, tgt_z, tgt)
    for dz in (2, 1, 3):
        z_copies[dz].wait_recv()
    here = piece(0, c, 0)
    add_rows(here, [here, z_in.at[0], z_in.at[1], z_in.at[2]])

    def y_part(dy):
        return mem.at[
            x, aligned(c * 128 + lax.rem(z, 2) * 64, 64),
            aligned(zh * SIDE + lax.rem(y + dy, 4) * FEATURES, FEATURES),
        ]

    y_copies = [remote(y_part(dy), y_in.at[dy - 1], dict(dy=dy)) for dy in (2, 1, 3)]
    ring_near(cot, tgt_in, tgt_z, tgt, tgt_far, grad_tokens)
    for copy in y_copies:
        copy.wait_recv()
    add_rows(grad_memory, [y_part(0), y_in.at[0], y_in.at[1], y_in.at[2]])
    flush()


def on_device(tokens, cotangent, memory, w_query, w_key, w_value, w_out):
    vmem = pltpu.VMEM
    scratch = [
        vmem((D, 2 * FEATURES), BF16),
        vmem((D, FEATURES), BF16),
        vmem((FEATURES, D), BF16),
        vmem((4, 256, D), BF16),
        vmem((TARGETS, D), BF16),
        vmem((TARGETS, D), BF16),
        vmem((MEMORY, 2 * FEATURES), BF16),
        vmem((MEMORY, 2 * FEATURES), BF16),
        vmem((TARGETS, FEATURES), BF16),
        vmem((TARGETS, FEATURES), BF16),
        vmem((TARGETS, FEATURES), BF16),
        vmem((TARGETS, FEATURES), BF16),
        vmem((TARGETS, MEMORY), F32),
        vmem((HEADS, TARGETS, MEMORY), BF16),
        vmem((HEADS, TARGETS, MEMORY), BF16),
        vmem((4, 128, D), BF16),
        vmem((2, 2, OWN_ROWS, SIDE), BF16),
        vmem((2, 4, OWN_ROWS, SIDE), BF16),
        vmem((3, OWN_ROWS, SIDE), BF16),
        vmem((3, OWN_ROWS, FEATURES), BF16),
        vmem((6, TARGETS, FEATURES), BF16),
        vmem((TARGETS, FEATURES), BF16),
        vmem((6, TARGETS, FEATURES), BF16),
        vmem((TARGETS, FEATURES), BF16),
        pltpu.SemaphoreType.DMA((N_SEMS,)),
        pltpu.SemaphoreType.DMA((N_SEMS,)),
        pltpu.SemaphoreType.DMA((N_LOCAL,)),
    ]
    return pl.pallas_call(
        kernel,
        out_shape=(
            jax.ShapeDtypeStruct(tokens.shape, BF16),
            jax.ShapeDtypeStruct(cotangent.shape, BF16),
            jax.ShapeDtypeStruct(memory.shape, BF16),
        ),
        in_specs=[pl.BlockSpec(memory_space=pl.ANY)] * 7,
        out_specs=(pl.BlockSpec(memory_space=pltpu.VMEM),) * 3,
        scratch_shapes=scratch,
        compiler_params=pltpu.CompilerParams(
            collective_id=0, has_side_effects=True, vmem_limit_bytes=62 * 2**20
        ),
        cost_estimate=pl.CostEstimate(flops=23 * 10**9, bytes_accessed=18 * 2**20, transcendentals=2**19),
    )(tokens, cotangent, memory, w_query, w_key, w_value, w_out)


def solution(mesh):
    placed = (
        P("section", None, "tp"),
        P("section", None, "tp"),
        P("section", "tp"),
        P("section", None, "tp"),
        P("section", None, "tp"),
        P("section", None, "tp"),
        P("section", "tp", None),
    )
    return jax.shard_map(
        on_device,
        mesh=mesh,
        in_specs=placed,
        out_specs=(P("section", None, "tp"), P("section", None, "tp"), P("section", "tp")),
        check_vma=False,
    )
```

```python
import functools

import jax
import jax.numpy as jnp
from jax import lax
from jax.experimental import pallas as pl
from jax.experimental.pallas import tpu as pltpu
from jax.sharding import PartitionSpec as P

HEAD_SIZE = 256
HEADS = 2
FEATURES = 512
D = 4096
TARGETS = 256
MEMORY = 1024
OWN_ROWS = 64
SIDE = 2048
SCALE = HEAD_SIZE ** -0.5
BF16 = jnp.bfloat16
F32 = jnp.float32
N_SEMS = 128
N_LOCAL = 48


def dot(a, b):
    return lax.dot_general(a, b, (((1,), (0,)), ((), ())), preferred_element_type=F32)


def dot_nt(a, b):
    return lax.dot_general(a, b, (((1,), (1,)), ((), ())), preferred_element_type=F32)


def dot_tn(a, b):
    return lax.dot_general(a, b, (((0,), (0,)), ((), ())), preferred_element_type=F32)


def aligned(start, size):
    return pl.ds(pl.multiple_of(start, size), size)


def add_rows(dst, srcs):
    rows = dst.shape[0]

    def step(i, _):
        part = aligned(i * 16, 16)
        total = srcs[0][part, :].astype(F32)
        for src in srcs[1:]:
            total = total + src[part, :].astype(F32)
        dst[part, :] = total.astype(dst.dtype)
        return 0

    lax.fori_loop(0, rows // 16, step, 0)


def kernel(
    tokens, cotangent, memory, w_query, w_key, w_value, w_out,
    attended, grad_tokens, grad_memory,
    wkv, wq, wo, mem, tok, cot, kv, gkv, queries_acc, gctx_acc, queries, gctx, ctx, gq, probs, probs_b, dscores,
    core_in, opposite_in, relay_in, final_in, z_in, y_in, att_in, att_z, tgt_in, tgt_z,
    send_sem, recv_sem, local_sem,
):
    section = lax.axis_index("section")
    tp = lax.axis_index("tp")
    c = lax.rem(section, 2)
    x = lax.rem(section // 2, 4)
    y = tp // 2
    zh = lax.rem(tp, 2)
    z = zh * 2 + section // 8

    def device(dx=0, dy=0, dz=0, dc=0):
        to_x, to_y, to_z = lax.rem(x + dx, 4), lax.rem(y + dy, 4), lax.rem(z + dz, 4)
        to_c = lax.rem(c + dc, 2)
        return ((lax.rem(to_z, 2) * 4 + to_x) * 2 + to_c, to_y * 2 + to_z // 2)

    counter = [0, 0]
    sends = []

    def remote(src, dst, where):
        i = counter[0]
        counter[0] += 1
        copy = pltpu.make_async_remote_copy(
            src_ref=src, dst_ref=dst, send_sem=send_sem.at[i], recv_sem=recv_sem.at[i],
            device_id=device(**where), device_id_type=pl.DeviceIdType.MESH,
        )
        copy.start()
        sends.append(copy)
        return copy

    def local(src, dst):
        i = counter[1]
        counter[1] += 1
        copy = pltpu.make_async_copy(src, dst, local_sem.at[i])
        copy.start()
        return copy

    def flush():
        for copy in sends:
            copy.wait_send()
        sends.clear()

    XP, XM, YP, YM = dict(dx=1), dict(dx=3), dict(dy=1), dict(dy=3)
    CORE, ZFAR = dict(dc=1), dict(dz=2)

    def x_at(dx):
        return lax.rem(x + dx, 4)

    def side(high):
        return aligned(high * SIDE, SIDE)

    def piece(dx, core, dz, half=None):
        to_z = lax.rem(z + dz, 4)
        row = core * 128 + lax.rem(to_z, 2) * 64
        rows = aligned(row, 64) if half is None else aligned(row + half * 32, 32)
        return mem.at[x_at(dx), rows, side(to_z // 2)]

    def block(buf, high, dy):
        return buf.at[:, aligned(high * SIDE + lax.rem(y + dy, 4) * FEATURES, FEATURES)]

    own_mem = mem.at[x, aligned(c * 128 + lax.rem(z, 2) * 64, 64), aligned(zh * SIDE + y * FEATURES, FEATURES)]
    near, far = zh, 1 - zh

    mem_load = local(memory, own_mem)
    tok_load = local(tokens.at[0], block(tok, near, 0))
    cot_load = local(cotangent.at[0], block(cot, near, 0))
    barrier = pltpu.get_barrier_semaphore()
    peers = [XP, XM, YP, YM, dict(dy=2), dict(dz=1), dict(dz=3), ZFAR, CORE]
    for where in peers:
        pl.semaphore_signal(barrier, inc=1, device_id=device(**where), device_id_type=pl.DeviceIdType.MESH)
    pl.semaphore_wait(barrier, len(peers))

    mem_y = {dy: remote(memory, own_mem, dict(dy=dy)) for dy in (1, 3, 2)}
    right, left, core_own, mem_z = {}, {}, {}, {}
    right[0] = [remote(memory, own_mem, XP)]
    left[0] = [remote(memory, own_mem, XM)]
    mem_z[1] = [remote(memory, own_mem, dict(dz=1))]
    mem_z[3] = [remote(memory, own_mem, dict(dz=3))]
    tok_z = remote(tokens.at[0], block(tok, near, 0), ZFAR)
    mem_load.wait()
    for dy in (1, 3, 2):
        mem_y[dy].wait_recv()
        here = mem.at[
            x, aligned(c * 128 + lax.rem(z, 2) * 64, 64), aligned(zh * SIDE + lax.rem(y + 4 - dy, 4) * FEATURES, FEATURES)
        ]
        right[0].append(remote(here, here, XP))
        left[0].append(remote(here, here, XM))
        mem_z[1].append(remote(here, here, dict(dz=1)))
        mem_z[3].append(remote(here, here, dict(dz=3)))
    own = piece(0, c, 0)
    core_right, core_left, core_opposite = {}, {}, {}
    on_right, on_left = {}, {}

    def spread(dz):
        here = piece(0, c, dz)
        right[dz] = [remote(here, here, XP)]
        left[dz] = [remote(here, here, XM)]
        core_own[dz] = remote(here, here, CORE)

    def spread_targets():
        t, g = tokens.at[0], cotangent.at[0]
        t_dst, g_dst = block(tok, near, 0), block(cot, near, 0)
        t_right = remote(t, t_dst, YP)
        g_left = remote(g, g_dst, YM)
        g_right = remote(g, g_dst, YP)
        t_left = remote(t, t_dst, YM)
        return t_right, g_left, g_right, t_left

    def spread_far(buf):
        here = block(buf, far, 0)
        return remote(here, here, YP), remote(here, here, YM)

    def arrive_x(dz):
        for copy in right[dz]:
            copy.wait_recv()
        if dz in (0, 2):
            on_right[dz] = remote(piece(3, c, dz, 0), piece(3, c, dz, 0), XP)
        core_left[dz] = remote(piece(3, c, dz), piece(3, c, dz), CORE)
        for copy in left[dz]:
            copy.wait_recv()
        if dz in (0, 2):
            on_left[dz] = remote(piece(1, c, dz, 1), piece(1, c, dz, 1), XM)
        core_right[dz] = remote(piece(1, c, dz), piece(1, c, dz), CORE)

    def arrive_opposite(dz):
        on_right[dz].wait_recv()
        a = remote(piece(2, c, dz, 0), piece(2, c, dz, 0), CORE)
        on_left[dz].wait_recv()
        b = remote(piece(2, c, dz, 1), piece(2, c, dz, 1), CORE)
        core_opposite[dz] = (a, b)

    def arrive_opposite_z(dz):
        opposite_z[4 - dz].wait_recv()
        core_opposite[dz] = (remote(piece(2, c, dz), piece(2, c, dz), CORE),)

    def forward_targets(high, ring):
        t_right, g_left, g_right, t_left = ring
        t_right.wait_recv()
        t_on = remote(block(tok, high, 3), block(tok, high, 3), YP)
        g_left.wait_recv()
        g_on = remote(block(cot, high, 1), block(cot, high, 1), YM)
        return t_on, g_on

    def keys_values(dx):
        to_x = x_at(dx)
        rows = aligned(to_x * 256, 256)

        def step(n, _):
            cols = aligned(n * 256, 256)
            kv[rows, cols] = dot(mem[to_x], wkv[:, cols]).astype(BF16)
            return 0

        lax.fori_loop(0, 4, step, 0)

    core_own[0] = remote(own, own, CORE)
    near_ring = spread_targets()
    kv_loads, q_loads, o_loads = [], [], []
    for high in range(2):
        for row in range(4):
            src = pl.ds((row * 2 + high) * FEATURES, FEATURES)
            dst = pl.ds(high * SIDE + row * FEATURES, FEATURES)
            kv_loads.append(local(w_key.at[0, src, :], wkv.at[dst, pl.ds(0, FEATURES)]))
            kv_loads.append(local(w_value.at[0, src, :], wkv.at[dst, pl.ds(FEATURES, FEATURES)]))
    tok_z.wait_recv()
    far_tok = spread_far(tok)
    arrive_x(0)
    for dz in (1, 3):
        for copy in mem_z[4 - dz]:
            copy.wait_recv()
        spread(dz)
    mem_z[2] = remote(own, own, ZFAR)
    cot_z = remote(cotangent.at[0], block(cot, near, 0), ZFAR)
    for high in range(2):
        for row in range(4):
            src = pl.ds((row * 2 + high) * FEATURES, FEATURES)
            dst = pl.ds(high * SIDE + row * FEATURES, FEATURES)
            q_loads.append(local(w_query.at[0, src, :], wq.at[dst, :]))
            o_loads.append(local(w_out.at[0, :, src], wo.at[:, dst]))

    near_on = forward_targets(near, near_ring)
    arrive_opposite(0)
    opposite_z = {dz: remote(piece(2, c, 0), piece(2, c, 0), dict(dz=dz)) for dz in (1, 3)}
    mem_z[2].wait_recv()
    spread(2)
    cot_z.wait_recv()
    far_cot = spread_far(cot)
    for copy in kv_loads:
        copy.wait()
    for dz in (0, 1, 3, 2):
        core_own[dz].wait_recv()
    keys_values(0)
    arrive_x(1)
    arrive_x(3)
    far_tok[0].wait_recv()
    far_t_on = remote(block(tok, far, 3), block(tok, far, 3), YP)

    def complete(ring, on):
        t_right, g_left, g_right, t_left = ring
        g_right.wait_recv()
        t_left.wait_recv()
        on[0].wait_recv()
        on[1].wait_recv()

    complete(near_ring, near_on)
    tok_load.wait()
    cot_load.wait()
    for copy in q_loads:
        copy.wait()
    for copy in o_loads:
        copy.wait()

    def project_near(n, _):
        cols = aligned(n * 256, 256)
        queries_acc[:, cols] = dot(tok[:, side(near)], wq[side(near), cols])
        gctx_acc[:, cols] = dot_nt(cot[:, side(near)], wo[cols, side(near)])
        return 0

    lax.fori_loop(0, 2, project_near, 0)
    arrive_opposite_z(1)
    arrive_opposite_z(3)
    arrive_x(2)
    far_cot[1].wait_recv()
    far_g_on = remote(block(cot, far, 1), block(cot, far, 1), YM)
    far_on = (far_t_on, far_g_on)
    far_ring = (far_tok[0], far_cot[1], far_cot[0], far_tok[1])
    arrive_opposite(2)
    for dz in (0, 1, 3, 2):
        core_right[dz].wait_recv()
    keys_values(1)
    for dz in (0, 1, 3, 2):
        core_left[dz].wait_recv()
    keys_values(3)
    for dz in (0, 1, 3, 2):
        for copy in core_opposite[dz]:
            copy.wait_recv()
    keys_values(2)
    complete(far_ring, far_on)

    def project_far(n, _):
        cols = aligned(n * 256, 256)
        queries[:, cols] = (queries_acc[:, cols] + dot(tok[:, side(far)], wq[side(far), cols])).astype(BF16)
        gctx[:, cols] = (gctx_acc[:, cols] + dot_nt(cot[:, side(far)], wo[cols, side(far)])).astype(BF16)
        return 0

    lax.fori_loop(0, 2, project_far, 0)
    flush()

    for h in range(HEADS):
        k_cols = pl.ds(h * HEAD_SIZE, HEAD_SIZE)
        v_cols = pl.ds(FEATURES + h * HEAD_SIZE, HEAD_SIZE)
        scores = dot_nt(queries[:, k_cols], kv[:, k_cols]) * SCALE
        top = jnp.max(scores, axis=-1, keepdims=True)
        weights = jnp.exp(scores - top)
        p = weights / jnp.sum(weights, axis=-1, keepdims=True)
        probs[...] = p
        p_b = p.astype(BF16)
        probs_b[h] = p_b
        grad_probs = dot_nt(gctx[:, k_cols], kv[:, v_cols])
        p = probs[...]
        delta = jnp.sum(grad_probs * p, axis=-1, keepdims=True)
        ds = (p * (grad_probs - delta) * SCALE).astype(BF16)
        dscores[h] = ds
        gkv[:, k_cols] = dot_tn(ds, queries[:, k_cols]).astype(BF16)
        gkv[:, v_cols] = dot_tn(probs_b[h], gctx[:, k_cols]).astype(BF16)

    def memory_terms(dx, high):
        to_x = x_at(dx)
        rows = aligned(to_x * 256, 256)

        def step(n, _):
            cols = aligned(high * SIDE + n * 512, 512)
            mem[to_x, :, cols] = dot_nt(gkv[rows, :], wkv[cols, :]).astype(BF16)
            return 0

        lax.fori_loop(0, 4, step, 0)
        return remote(
            mem.at[to_x, aligned((1 - c) * 128, 128), side(high)], core_in.at[to_x, :, side(high)], CORE
        )

    zl = lax.rem(z, 2)

    def part(dx, high, low):
        return mem.at[x_at(dx), aligned(c * 128 + low * 64, 64), side(high)]

    def pair_sum(dx, high, low, extra=()):
        here = part(dx, high, low)
        other = core_in.at[x_at(dx), aligned(low * 64, 64), side(high)]
        add_rows(here, [here, other] + list(extra))
        return here

    def far_relay(buf, inbox):
        return remote(block(buf, far, 2), inbox.at[0], YP)

    def near_relay(buf, inbox):
        return remote(block(buf, near, 2), inbox.at[1], YM)

    def far_on_left(buf, inbox, terms):
        terms(far, 3)
        return remote(block(buf, far, 3), inbox.at[3], YM)

    def near_on_right(buf, inbox, terms):
        terms(near, 1)
        return remote(block(buf, near, 1), inbox.at[2], YP)

    def far_on_right(buf, inbox, a_relay):
        a_relay.wait_recv()
        here = block(buf, far, 1)
        add_rows(here, [here, inbox.at[0]])
        return remote(here, inbox.at[4], YP)

    def near_on_left(buf, inbox, b_relay):
        b_relay.wait_recv()
        here = block(buf, near, 3)
        add_rows(here, [here, inbox.at[1]])
        return remote(here, inbox.at[5], YM)

    def ring_far(buf, inbox, z_box, a_left, a_right):
        a_left.wait_recv()
        a_right.wait_recv()
        here = block(buf, far, 0)
        add_rows(here, [here, inbox.at[3], inbox.at[4]])
        return remote(here, z_box, ZFAR)

    def ring_near(buf, inbox, z_box, b_right, b_left, z_copy, out):
        b_right.wait_recv()
        b_left.wait_recv()
        z_copy.wait_recv()
        add_rows(out.at[0], [block(buf, near, 0), inbox.at[2], inbox.at[5], z_box])

    def out_terms(high, dy):
        cols = aligned(high * SIDE + lax.rem(y + dy, 4) * FEATURES, FEATURES)
        tok[:, cols] = dot(ctx[...], wo[:, cols]).astype(BF16)

    def target_terms(high, dy):
        rows = aligned(high * SIDE + lax.rem(y + dy, 4) * FEATURES, FEATURES)
        cot[:, rows] = dot_nt(gq[...], wq[rows, :]).astype(BF16)

    lows = (zl, 1 - zl)
    far_lows, near_lows = lows, lows[::-1]

    def x_final_far(i):
        far_left[i].wait_recv()
        far_right[i].wait_recv()
        here = pair_sum(0, far, far_lows[i], [final_in.at[0, i], final_in.at[1, i]])
        if i == 0:
            return remote(here, z_in.at[0], ZFAR)
        return remote(here, z_in.at[1], dict(dz=3 - 2 * zl))

    def x_final_near(i):
        near_right[i].wait_recv()
        near_left[i].wait_recv()
        here = pair_sum(0, near, near_lows[i], [final_in.at[0, 2 + i], final_in.at[1, 2 + i]])
        if i == 0:
            return remote(here, z_in.at[2], dict(dz=1 + 2 * zl))
        return here

    core_2f = memory_terms(2, far)
    core_3f = memory_terms(3, far)
    for h in range(HEADS):
        cols = pl.ds(h * HEAD_SIZE, HEAD_SIZE)
        v_cols = pl.ds(FEATURES + h * HEAD_SIZE, HEAD_SIZE)
        ctx[:, cols] = dot(probs_b[h], kv[:, v_cols]).astype(BF16)
    out_terms(far, 2)
    att_far_relay = far_relay(tok, att_in)
    att_far_left = far_on_left(tok, att_in, out_terms)
    core_2f.wait_recv()
    opposite_far = remote(pair_sum(2, far, 1 - zl), opposite_in.at[1], dict(dz=3 - 2 * zl))
    relay_right = remote(pair_sum(2, far, zl), relay_in.at[0], XP)
    core_2n = memory_terms(2, near)
    core_3f.wait_recv()
    far_left = [remote(pair_sum(3, far, zl), final_in.at[1, 0], XM)]
    for h in range(HEADS):
        cols = pl.ds(h * HEAD_SIZE, HEAD_SIZE)
        gq[:, cols] = dot(dscores[h], kv[:, cols]).astype(BF16)
    out_terms(far, 1)
    target_terms(far, 2)
    core_1f = memory_terms(1, far)
    core_2n.wait_recv()
    opposite_near = remote(pair_sum(2, near, 1 - zl), opposite_in.at[0], dict(dz=1 + 2 * zl))
    target_terms(far, 1)
    far_left.append(remote(pair_sum(3, far, 1 - zl), final_in.at[1, 1], XM))
    core_1n = memory_terms(1, near)
    out_terms(near, 2)
    att_far_right = far_on_right(tok, att_in, att_far_relay)
    tgt_far_relay = far_relay(cot, tgt_in)
    tgt_far_left = far_on_left(cot, tgt_in, target_terms)
    core_1f.wait_recv()
    relay_right.wait_recv()
    far_right = [remote(pair_sum(1, far, zl, [relay_in.at[0]]), final_in.at[0, 0], XP)]
    opposite_near.wait_recv()
    opposite_far.wait_recv()
    relay_left = remote(
        pair_sum(2, near, zl, [opposite_in.at[0], opposite_in.at[1]]), relay_in.at[1], XM
    )
    att_near_relay = near_relay(tok, att_in)
    core_0f = memory_terms(0, far)
    far_right.append(remote(pair_sum(1, far, 1 - zl), final_in.at[0, 1], XP))
    out_terms(far, 0)
    core_3n = memory_terms(3, near)
    target_terms(near, 2)
    core_0f.wait_recv()
    att_far = ring_far(tok, att_in, att_z, att_far_left, att_far_right)
    z_far0 = x_final_far(0)
    core_1n.wait_recv()
    near_right = [remote(pair_sum(1, near, 1 - zl), final_in.at[0, 2], XP)]
    core_3n.wait_recv()
    near_left = [remote(pair_sum(3, near, 1 - zl), final_in.at[1, 2], XM)]
    tgt_near_relay = near_relay(cot, tgt_in)
    att_near_right = near_on_right(tok, att_in, out_terms)
    target_terms(far, 0)
    out_terms(near, 3)
    target_terms(near, 3)
    tgt_far_right = far_on_right(cot, tgt_in, tgt_far_relay)
    z_far1 = x_final_far(1)
    near_right.append(remote(pair_sum(1, near, zl), final_in.at[0, 3], XP))
    relay_left.wait_recv()
    near_left.append(remote(pair_sum(3, near, zl, [relay_in.at[1]]), final_in.at[1, 3], XM))
    tgt_near_right = near_on_right(cot, tgt_in, target_terms)
    att_near_left = near_on_left(tok, att_in, att_near_relay)
    core_0n = memory_terms(0, near)
    out_terms(near, 0)
    target_terms(near, 0)
    core_0n.wait_recv()
    tgt_near_left = near_on_left(cot, tgt_in, tgt_near_relay)
    z_near0 = x_final_near(0)
    tgt_far = ring_far(cot, tgt_in, tgt_z, tgt_far_left, tgt_far_right)
    here = x_final_near(1)
    for copy in (z_far0, z_near0, z_far1):
        copy.wait_recv()
    add_rows(here, [here, z_in.at[0], z_in.at[1], z_in.at[2]])

    def y_part(dy):
        return mem.at[
            x, aligned(c * 128 + zl * 64, 64), aligned(zh * SIDE + lax.rem(y + dy, 4) * FEATURES, FEATURES)
        ]

    y_copies = [remote(y_part(dy), y_in.at[dy - 1], dict(dy=dy)) for dy in (2, 1, 3)]
    ring_near(tok, att_in, att_z, att_near_right, att_near_left, att_far, attended)
    ring_near(cot, tgt_in, tgt_z, tgt_near_right, tgt_near_left, tgt_far, grad_tokens)
    for copy in y_copies:
        copy.wait_recv()
    add_rows(grad_memory, [y_part(0), y_in.at[0], y_in.at[1], y_in.at[2]])
    flush()


def hand_over(a_in, b_in, c_in, a_out, b_out, c_out):
    a_out[...] = a_in[...]
    b_out[...] = b_in[...]
    c_out[...] = c_in[...]


def on_device(tokens, cotangent, memory, w_query, w_key, w_value, w_out):
    vmem = pltpu.VMEM
    scratch = [
        vmem((D, 2 * FEATURES), BF16),
        vmem((D, FEATURES), BF16),
        vmem((FEATURES, D), BF16),
        vmem((4, 256, D), BF16),
        vmem((TARGETS, D), BF16),
        vmem((TARGETS, D), BF16),
        vmem((MEMORY, 2 * FEATURES), BF16),
        vmem((MEMORY, 2 * FEATURES), BF16),
        vmem((TARGETS, FEATURES), F32),
        vmem((TARGETS, FEATURES), F32),
        vmem((TARGETS, FEATURES), BF16),
        vmem((TARGETS, FEATURES), BF16),
        vmem((TARGETS, FEATURES), BF16),
        vmem((TARGETS, FEATURES), BF16),
        vmem((TARGETS, MEMORY), F32),
        vmem((HEADS, TARGETS, MEMORY), BF16),
        vmem((HEADS, TARGETS, MEMORY), BF16),
        vmem((4, 128, D), BF16),
        vmem((2, OWN_ROWS, SIDE), BF16),
        vmem((2, OWN_ROWS, SIDE), BF16),
        vmem((2, 4, OWN_ROWS, SIDE), BF16),
        vmem((3, OWN_ROWS, SIDE), BF16),
        vmem((3, OWN_ROWS, FEATURES), BF16),
        vmem((6, TARGETS, FEATURES), BF16),
        vmem((TARGETS, FEATURES), BF16),
        vmem((6, TARGETS, FEATURES), BF16),
        vmem((TARGETS, FEATURES), BF16),
        pltpu.SemaphoreType.DMA((N_SEMS,)),
        pltpu.SemaphoreType.DMA((N_SEMS,)),
        pltpu.SemaphoreType.DMA((N_LOCAL,)),
    ]
    results = pl.pallas_call(
        kernel,
        out_shape=(
            jax.ShapeDtypeStruct(tokens.shape, BF16),
            jax.ShapeDtypeStruct(cotangent.shape, BF16),
            jax.ShapeDtypeStruct(memory.shape, BF16),
        ),
        in_specs=[pl.BlockSpec(memory_space=pl.ANY)] * 7,
        out_specs=(pl.BlockSpec(memory_space=pltpu.VMEM),) * 3,
        scratch_shapes=scratch,
        compiler_params=pltpu.CompilerParams(
            collective_id=0, has_side_effects=True, vmem_limit_bytes=62 * 2**20
        ),
        cost_estimate=pl.CostEstimate(flops=23 * 10**9, bytes_accessed=18 * 2**20, transcendentals=2**19),
    )(tokens, cotangent, memory, w_query, w_key, w_value, w_out)
    return pl.pallas_call(
        hand_over,
        out_shape=tuple(jax.ShapeDtypeStruct(r.shape, r.dtype) for r in results),
        in_specs=[pl.BlockSpec(memory_space=pltpu.VMEM)] * 3,
        out_specs=(pl.BlockSpec(memory_space=pltpu.VMEM),) * 3,
    )(*results)


def solution(mesh):
    placed = (
        P("section", None, "tp"),
        P("section", None, "tp"),
        P("section", "tp"),
        P("section", None, "tp"),
        P("section", None, "tp"),
        P("section", None, "tp"),
        P("section", "tp", None),
    )
    return jax.shard_map(
        on_device,
        mesh=mesh,
        in_specs=placed,
        out_specs=(P("section", None, "tp"), P("section", None, "tp"), P("section", "tp")),
        check_vma=False,
    )
```

```python
import functools

import jax
import jax.numpy as jnp
from jax import lax
from jax.experimental import pallas as pl
from jax.experimental.pallas import tpu as pltpu
from jax.sharding import PartitionSpec as P

HEAD_SIZE = 256
HEADS = 2
FEATURES = 512
D = 4096
TARGETS = 256
MEMORY = 1024
OWN_ROWS = 64
SIDE = 2048
SCALE = HEAD_SIZE ** -0.5
BF16 = jnp.bfloat16
F32 = jnp.float32
N_SEMS = 128
N_LOCAL = 48


def dot(a, b):
    return lax.dot_general(a, b, (((1,), (0,)), ((), ())), preferred_element_type=F32)


def dot_nt(a, b):
    return lax.dot_general(a, b, (((1,), (1,)), ((), ())), preferred_element_type=F32)


def dot_tn(a, b):
    return lax.dot_general(a, b, (((0,), (0,)), ((), ())), preferred_element_type=F32)


def aligned(start, size):
    return pl.ds(pl.multiple_of(start, size), size)


def add_rows(dst, srcs):
    rows = dst.shape[0]

    def step(i, _):
        part = aligned(i * 16, 16)
        total = srcs[0][part, :].astype(F32)
        for src in srcs[1:]:
            total = total + src[part, :].astype(F32)
        dst[part, :] = total.astype(dst.dtype)
        return 0

    lax.fori_loop(0, rows // 16, step, 0)


def kernel(
    tokens, cotangent, memory, w_query, w_key, w_value, w_out,
    attended, grad_tokens, grad_memory,
    wkv, wq, wo, mem, tok, cot, kv, gkv, queries_acc, gctx_acc, queries, gctx, ctx, gq, probs, probs_b, dscores,
    core_in, opposite_in, relay_in, final_in, z_in, y_in, att_in, att_z, tgt_in, tgt_z,
    send_sem, recv_sem, local_sem,
):
    section = lax.axis_index("section")
    tp = lax.axis_index("tp")
    c = lax.rem(section, 2)
    x = lax.rem(section // 2, 4)
    y = tp // 2
    zh = lax.rem(tp, 2)
    z = zh * 2 + section // 8

    def device(dx=0, dy=0, dz=0, dc=0):
        to_x, to_y, to_z = lax.rem(x + dx, 4), lax.rem(y + dy, 4), lax.rem(z + dz, 4)
        to_c = lax.rem(c + dc, 2)
        return ((lax.rem(to_z, 2) * 4 + to_x) * 2 + to_c, to_y * 2 + to_z // 2)

    counter = [0, 0]
    sends = []

    def remote(src, dst, where):
        i = counter[0]
        counter[0] += 1
        copy = pltpu.make_async_remote_copy(
            src_ref=src, dst_ref=dst, send_sem=send_sem.at[i], recv_sem=recv_sem.at[i],
            device_id=device(**where), device_id_type=pl.DeviceIdType.MESH,
        )
        copy.start()
        sends.append(copy)
        return copy

    def local(src, dst):
        i = counter[1]
        counter[1] += 1
        copy = pltpu.make_async_copy(src, dst, local_sem.at[i])
        copy.start()
        return copy

    def flush():
        for copy in sends:
            copy.wait_send()
        sends.clear()

    XP, XM, YP, YM = dict(dx=1), dict(dx=3), dict(dy=1), dict(dy=3)
    CORE, ZFAR = dict(dc=1), dict(dz=2)

    def x_at(dx):
        return lax.rem(x + dx, 4)

    def side(high):
        return aligned(high * SIDE, SIDE)

    def piece(dx, core, dz, half=None):
        to_z = lax.rem(z + dz, 4)
        row = core * 128 + lax.rem(to_z, 2) * 64
        rows = aligned(row, 64) if half is None else aligned(row + half * 32, 32)
        return mem.at[x_at(dx), rows, side(to_z // 2)]

    def block(buf, high, dy):
        return buf.at[:, aligned(high * SIDE + lax.rem(y + dy, 4) * FEATURES, FEATURES)]

    own_mem = mem.at[x, aligned(c * 128 + lax.rem(z, 2) * 64, 64), aligned(zh * SIDE + y * FEATURES, FEATURES)]
    near, far = zh, 1 - zh

    mem_load = local(memory, own_mem)
    tok_load = local(tokens.at[0], block(tok, near, 0))
    cot_load = local(cotangent.at[0], block(cot, near, 0))
    barrier = pltpu.get_barrier_semaphore()
    peers = [XP, XM, YP, YM, dict(dy=2), dict(dz=1), dict(dz=3), ZFAR, CORE]
    for where in peers:
        pl.semaphore_signal(barrier, inc=1, device_id=device(**where), device_id_type=pl.DeviceIdType.MESH)
    pl.semaphore_wait(barrier, len(peers))

    mem_y = {dy: remote(memory, own_mem, dict(dy=dy)) for dy in (1, 3, 2)}
    right, left, core_own, mem_z = {}, {}, {}, {}
    right[0] = [remote(memory, own_mem, XP)]
    left[0] = [remote(memory, own_mem, XM)]
    mem_z[1] = [remote(memory, own_mem, dict(dz=1))]
    mem_z[3] = [remote(memory, own_mem, dict(dz=3))]
    tok_z = remote(tokens.at[0], block(tok, near, 0), ZFAR)
    mem_load.wait()
    for dy in (1, 3, 2):
        mem_y[dy].wait_recv()
        here = mem.at[
            x, aligned(c * 128 + lax.rem(z, 2) * 64, 64), aligned(zh * SIDE + lax.rem(y + 4 - dy, 4) * FEATURES, FEATURES)
        ]
        right[0].append(remote(here, here, XP))
        left[0].append(remote(here, here, XM))
        mem_z[1].append(remote(here, here, dict(dz=1)))
        mem_z[3].append(remote(here, here, dict(dz=3)))
    own = piece(0, c, 0)
    core_right, core_left, core_opposite = {}, {}, {}
    on_right, on_left = {}, {}

    def spread(dz):
        here = piece(0, c, dz)
        right[dz] = [remote(here, here, XP)]
        left[dz] = [remote(here, here, XM)]
        core_own[dz] = remote(here, here, CORE)

    def spread_targets():
        t, g = tokens.at[0], cotangent.at[0]
        t_dst, g_dst = block(tok, near, 0), block(cot, near, 0)
        t_right = remote(t, t_dst, YP)
        g_left = remote(g, g_dst, YM)
        g_right = remote(g, g_dst, YP)
        t_left = remote(t, t_dst, YM)
        return t_right, g_left, g_right, t_left

    def spread_far(buf):
        here = block(buf, far, 0)
        return remote(here, here, YP), remote(here, here, YM)

    def arrive_x(dz):
        for copy in right[dz]:
            copy.wait_recv()
        if dz in (0, 2):
            on_right[dz] = remote(piece(3, c, dz, 0), piece(3, c, dz, 0), XP)
        core_left[dz] = remote(piece(3, c, dz), piece(3, c, dz), CORE)
        for copy in left[dz]:
            copy.wait_recv()
        if dz in (0, 2):
            on_left[dz] = remote(piece(1, c, dz, 1), piece(1, c, dz, 1), XM)
        core_right[dz] = remote(piece(1, c, dz), piece(1, c, dz), CORE)

    def arrive_opposite(dz):
        on_right[dz].wait_recv()
        a = remote(piece(2, c, dz, 0), piece(2, c, dz, 0), CORE)
        on_left[dz].wait_recv()
        b = remote(piece(2, c, dz, 1), piece(2, c, dz, 1), CORE)
        core_opposite[dz] = (a, b)

    def arrive_opposite_z(dz):
        opposite_z[4 - dz].wait_recv()
        core_opposite[dz] = (remote(piece(2, c, dz), piece(2, c, dz), CORE),)

    def forward_targets(high, ring):
        t_right, g_left, g_right, t_left = ring
        t_right.wait_recv()
        t_on = remote(block(tok, high, 3), block(tok, high, 3), YP)
        g_left.wait_recv()
        g_on = remote(block(cot, high, 1), block(cot, high, 1), YM)
        return t_on, g_on

    def keys_values(dx):
        to_x = x_at(dx)
        rows = aligned(to_x * 256, 256)

        def step(n, _):
            cols = aligned(n * 512, 512)
            kv[rows, cols] = dot(mem[to_x], wkv[:, cols]).astype(BF16)
            return 0

        lax.fori_loop(0, 2, step, 0)

    core_own[0] = remote(own, own, CORE)
    near_ring = spread_targets()
    kv_loads, q_loads, o_loads = [], [], []
    for high in range(2):
        for row in range(4):
            src = pl.ds((row * 2 + high) * FEATURES, FEATURES)
            dst = pl.ds(high * SIDE + row * FEATURES, FEATURES)
            kv_loads.append(local(w_key.at[0, src, :], wkv.at[dst, pl.ds(0, FEATURES)]))
            kv_loads.append(local(w_value.at[0, src, :], wkv.at[dst, pl.ds(FEATURES, FEATURES)]))
    tok_z.wait_recv()
    far_tok = spread_far(tok)
    arrive_x(0)
    for dz in (1, 3):
        for copy in mem_z[4 - dz]:
            copy.wait_recv()
        spread(dz)
    mem_z[2] = remote(own, own, ZFAR)
    cot_z = remote(cotangent.at[0], block(cot, near, 0), ZFAR)
    for high in range(2):
        for row in range(4):
            src = pl.ds((row * 2 + high) * FEATURES, FEATURES)
            dst = pl.ds(high * SIDE + row * FEATURES, FEATURES)
            q_loads.append(local(w_query.at[0, src, :], wq.at[dst, :]))
            o_loads.append(local(w_out.at[0, :, src], wo.at[:, dst]))

    near_on = forward_targets(near, near_ring)
    arrive_opposite(0)
    opposite_z = {dz: remote(piece(2, c, 0), piece(2, c, 0), dict(dz=dz)) for dz in (1, 3)}
    mem_z[2].wait_recv()
    spread(2)
    cot_z.wait_recv()
    far_cot = spread_far(cot)
    for copy in kv_loads:
        copy.wait()
    for dz in (0, 1, 3, 2):
        core_own[dz].wait_recv()
    keys_values(0)
    arrive_x(1)
    arrive_x(3)
    far_tok[0].wait_recv()
    far_t_on = remote(block(tok, far, 3), block(tok, far, 3), YP)

    def complete(ring, on):
        t_right, g_left, g_right, t_left = ring
        g_right.wait_recv()
        t_left.wait_recv()
        on[0].wait_recv()
        on[1].wait_recv()

    complete(near_ring, near_on)
    tok_load.wait()
    cot_load.wait()
    for copy in q_loads:
        copy.wait()
    for copy in o_loads:
        copy.wait()

    def project_near():
        queries_acc[...] = dot(tok[:, side(near)], wq[side(near), :])
        gctx_acc[...] = dot_nt(cot[:, side(near)], wo[:, side(near)])

    project_near()
    arrive_opposite_z(1)
    arrive_opposite_z(3)
    arrive_x(2)
    far_cot[1].wait_recv()
    far_g_on = remote(block(cot, far, 1), block(cot, far, 1), YM)
    far_on = (far_t_on, far_g_on)
    far_ring = (far_tok[0], far_cot[1], far_cot[0], far_tok[1])
    for dz in (0, 1, 3, 2):
        core_right[dz].wait_recv()
    keys_values(1)
    arrive_opposite(2)
    for dz in (0, 1, 3, 2):
        core_left[dz].wait_recv()
    keys_values(3)
    for dz in (0, 1, 3, 2):
        for copy in core_opposite[dz]:
            copy.wait_recv()
    keys_values(2)
    complete(far_ring, far_on)

    def project_far():
        queries[...] = (queries_acc[...] + dot(tok[:, side(far)], wq[side(far), :])).astype(BF16)
        gctx[...] = (gctx_acc[...] + dot_nt(cot[:, side(far)], wo[:, side(far)])).astype(BF16)

    project_far()
    flush()

    for h in range(HEADS):
        k_cols = pl.ds(h * HEAD_SIZE, HEAD_SIZE)
        v_cols = pl.ds(FEATURES + h * HEAD_SIZE, HEAD_SIZE)
        scores = dot_nt(queries[:, k_cols], kv[:, k_cols]) * SCALE
        top = jnp.max(scores, axis=-1, keepdims=True)
        weights = jnp.exp(scores - top)
        p = weights / jnp.sum(weights, axis=-1, keepdims=True)
        probs[...] = p
        p_b = p.astype(BF16)
        probs_b[h] = p_b
        grad_probs = dot_nt(gctx[:, k_cols], kv[:, v_cols])
        p = probs[...]
        delta = jnp.sum(grad_probs * p, axis=-1, keepdims=True)
        ds = (p * (grad_probs - delta) * SCALE).astype(BF16)
        dscores[h] = ds
        gkv[:, k_cols] = dot_tn(ds, queries[:, k_cols]).astype(BF16)
        gkv[:, v_cols] = dot_tn(probs_b[h], gctx[:, k_cols]).astype(BF16)

    def memory_terms(dx, high):
        to_x = x_at(dx)
        rows = aligned(to_x * 256, 256)

        def step(n, _):
            cols = aligned(high * SIDE + n * 512, 512)
            mem[to_x, :, cols] = dot_nt(gkv[rows, :], wkv[cols, :]).astype(BF16)
            return 0

        lax.fori_loop(0, 4, step, 0)
        return remote(
            mem.at[to_x, aligned((1 - c) * 128, 128), side(high)], core_in.at[to_x, :, side(high)], CORE
        )

    zl = lax.rem(z, 2)

    def part(dx, high, low):
        return mem.at[x_at(dx), aligned(c * 128 + low * 64, 64), side(high)]

    def pair_sum(dx, high, low, extra=()):
        here = part(dx, high, low)
        other = core_in.at[x_at(dx), aligned(low * 64, 64), side(high)]
        add_rows(here, [here, other] + list(extra))
        return here

    def far_relay(buf, inbox):
        return remote(block(buf, far, 2), inbox.at[0], YP)

    def near_relay(buf, inbox):
        return remote(block(buf, near, 2), inbox.at[1], YM)

    def far_on_left(buf, inbox, terms):
        terms(far, 3)
        return remote(block(buf, far, 3), inbox.at[3], YM)

    def near_on_right(buf, inbox, terms):
        terms(near, 1)
        return remote(block(buf, near, 1), inbox.at[2], YP)

    def far_on_right(buf, inbox, a_relay):
        a_relay.wait_recv()
        here = block(buf, far, 1)
        add_rows(here, [here, inbox.at[0]])
        return remote(here, inbox.at[4], YP)

    def near_on_left(buf, inbox, b_relay):
        b_relay.wait_recv()
        here = block(buf, near, 3)
        add_rows(here, [here, inbox.at[1]])
        return remote(here, inbox.at[5], YM)

    def ring_far(buf, inbox, z_box, a_left, a_right):
        a_left.wait_recv()
        a_right.wait_recv()
        here = block(buf, far, 0)
        add_rows(here, [here, inbox.at[3], inbox.at[4]])
        return remote(here, z_box, ZFAR)

    def ring_near(buf, inbox, z_box, b_right, b_left, z_copy, out):
        b_right.wait_recv()
        b_left.wait_recv()
        z_copy.wait_recv()
        add_rows(out.at[0], [block(buf, near, 0), inbox.at[2], inbox.at[5], z_box])

    def out_terms(high, dy):
        cols = aligned(high * SIDE + lax.rem(y + dy, 4) * FEATURES, FEATURES)
        tok[:, cols] = dot(ctx[...], wo[:, cols]).astype(BF16)

    def target_terms(high, dy):
        rows = aligned(high * SIDE + lax.rem(y + dy, 4) * FEATURES, FEATURES)
        cot[:, rows] = dot_nt(gq[...], wq[rows, :]).astype(BF16)

    lows = (zl, 1 - zl)
    far_lows, near_lows = lows, lows[::-1]

    def x_final_far(i):
        far_left[i].wait_recv()
        far_right[i].wait_recv()
        here = pair_sum(0, far, far_lows[i], [final_in.at[0, i], final_in.at[1, i]])
        if i == 0:
            return remote(here, z_in.at[0], ZFAR)
        return remote(here, z_in.at[1], dict(dz=3 - 2 * zl))

    def x_final_near(i):
        near_right[i].wait_recv()
        near_left[i].wait_recv()
        here = pair_sum(0, near, near_lows[i], [final_in.at[0, 2 + i], final_in.at[1, 2 + i]])
        if i == 0:
            return remote(here, z_in.at[2], dict(dz=1 + 2 * zl))
        return here

    core_2f = memory_terms(2, far)
    core_3f = memory_terms(3, far)
    for h in range(HEADS):
        cols = pl.ds(h * HEAD_SIZE, HEAD_SIZE)
        v_cols = pl.ds(FEATURES + h * HEAD_SIZE, HEAD_SIZE)
        ctx[:, cols] = dot(probs_b[h], kv[:, v_cols]).astype(BF16)
    out_terms(far, 2)
    att_far_relay = far_relay(tok, att_in)
    att_far_left = far_on_left(tok, att_in, out_terms)
    core_2f.wait_recv()
    opposite_far = remote(pair_sum(2, far, 1 - zl), opposite_in.at[1], dict(dz=3 - 2 * zl))
    relay_right = remote(pair_sum(2, far, zl), relay_in.at[0], XP)
    core_2n = memory_terms(2, near)
    core_3f.wait_recv()
    far_left = [remote(pair_sum(3, far, zl), final_in.at[1, 0], XM)]
    for h in range(HEADS):
        cols = pl.ds(h * HEAD_SIZE, HEAD_SIZE)
        gq[:, cols] = dot(dscores[h], kv[:, cols]).astype(BF16)
    out_terms(far, 1)
    target_terms(far, 2)
    core_1f = memory_terms(1, far)
    core_2n.wait_recv()
    opposite_near = remote(pair_sum(2, near, 1 - zl), opposite_in.at[0], dict(dz=1 + 2 * zl))
    target_terms(far, 1)
    far_left.append(remote(pair_sum(3, far, 1 - zl), final_in.at[1, 1], XM))
    core_1n = memory_terms(1, near)
    out_terms(near, 2)
    att_far_right = far_on_right(tok, att_in, att_far_relay)
    tgt_far_relay = far_relay(cot, tgt_in)
    tgt_far_left = far_on_left(cot, tgt_in, target_terms)
    core_1f.wait_recv()
    relay_right.wait_recv()
    far_right = [remote(pair_sum(1, far, zl, [relay_in.at[0]]), final_in.at[0, 0], XP)]
    opposite_near.wait_recv()
    opposite_far.wait_recv()
    relay_left = remote(
        pair_sum(2, near, zl, [opposite_in.at[0], opposite_in.at[1]]), relay_in.at[1], XM
    )
    att_near_relay = near_relay(tok, att_in)
    core_0f = memory_terms(0, far)
    far_right.append(remote(pair_sum(1, far, 1 - zl), final_in.at[0, 1], XP))
    out_terms(far, 0)
    core_3n = memory_terms(3, near)
    target_terms(near, 2)
    core_0f.wait_recv()
    att_far = ring_far(tok, att_in, att_z, att_far_left, att_far_right)
    z_far0 = x_final_far(0)
    core_1n.wait_recv()
    near_right = [remote(pair_sum(1, near, 1 - zl), final_in.at[0, 2], XP)]
    core_3n.wait_recv()
    near_left = [remote(pair_sum(3, near, 1 - zl), final_in.at[1, 2], XM)]
    tgt_near_relay = near_relay(cot, tgt_in)
    att_near_right = near_on_right(tok, att_in, out_terms)
    target_terms(far, 0)
    out_terms(near, 3)
    target_terms(near, 3)
    tgt_far_right = far_on_right(cot, tgt_in, tgt_far_relay)
    z_far1 = x_final_far(1)
    near_right.append(remote(pair_sum(1, near, zl), final_in.at[0, 3], XP))
    relay_left.wait_recv()
    near_left.append(remote(pair_sum(3, near, zl, [relay_in.at[1]]), final_in.at[1, 3], XM))
    tgt_near_right = near_on_right(cot, tgt_in, target_terms)
    att_near_left = near_on_left(tok, att_in, att_near_relay)
    core_0n = memory_terms(0, near)
    out_terms(near, 0)
    target_terms(near, 0)
    core_0n.wait_recv()
    tgt_near_left = near_on_left(cot, tgt_in, tgt_near_relay)
    z_near0 = x_final_near(0)
    tgt_far = ring_far(cot, tgt_in, tgt_z, tgt_far_left, tgt_far_right)
    here = x_final_near(1)
    for copy in (z_far0, z_near0, z_far1):
        copy.wait_recv()
    add_rows(here, [here, z_in.at[0], z_in.at[1], z_in.at[2]])

    def y_part(dy):
        return mem.at[
            x, aligned(c * 128 + zl * 64, 64), aligned(zh * SIDE + lax.rem(y + dy, 4) * FEATURES, FEATURES)
        ]

    y_copies = [remote(y_part(dy), y_in.at[dy - 1], dict(dy=dy)) for dy in (2, 1, 3)]
    ring_near(tok, att_in, att_z, att_near_right, att_near_left, att_far, attended)
    ring_near(cot, tgt_in, tgt_z, tgt_near_right, tgt_near_left, tgt_far, grad_tokens)
    for copy in y_copies:
        copy.wait_recv()
    add_rows(grad_memory, [y_part(0), y_in.at[0], y_in.at[1], y_in.at[2]])
    flush()


def hand_over(a_in, b_in, c_in, a_out, b_out, c_out):
    a_out[...] = a_in[...]
    b_out[...] = b_in[...]
    c_out[...] = c_in[...]


def on_device(tokens, cotangent, memory, w_query, w_key, w_value, w_out):
    vmem = pltpu.VMEM
    scratch = [
        vmem((D, 2 * FEATURES), BF16),
        vmem((D, FEATURES), BF16),
        vmem((FEATURES, D), BF16),
        vmem((4, 256, D), BF16),
        vmem((TARGETS, D), BF16),
        vmem((TARGETS, D), BF16),
        vmem((MEMORY, 2 * FEATURES), BF16),
        vmem((MEMORY, 2 * FEATURES), BF16),
        vmem((TARGETS, FEATURES), F32),
        vmem((TARGETS, FEATURES), F32),
        vmem((TARGETS, FEATURES), BF16),
        vmem((TARGETS, FEATURES), BF16),
        vmem((TARGETS, FEATURES), BF16),
        vmem((TARGETS, FEATURES), BF16),
        vmem((TARGETS, MEMORY), F32),
        vmem((HEADS, TARGETS, MEMORY), BF16),
        vmem((HEADS, TARGETS, MEMORY), BF16),
        vmem((4, 128, D), BF16),
        vmem((2, OWN_ROWS, SIDE), BF16),
        vmem((2, OWN_ROWS, SIDE), BF16),
        vmem((2, 4, OWN_ROWS, SIDE), BF16),
        vmem((3, OWN_ROWS, SIDE), BF16),
        vmem((3, OWN_ROWS, FEATURES), BF16),
        vmem((6, TARGETS, FEATURES), BF16),
        vmem((TARGETS, FEATURES), BF16),
        vmem((6, TARGETS, FEATURES), BF16),
        vmem((TARGETS, FEATURES), BF16),
        pltpu.SemaphoreType.DMA((N_SEMS,)),
        pltpu.SemaphoreType.DMA((N_SEMS,)),
        pltpu.SemaphoreType.DMA((N_LOCAL,)),
    ]
    results = pl.pallas_call(
        kernel,
        out_shape=(
            jax.ShapeDtypeStruct(tokens.shape, BF16),
            jax.ShapeDtypeStruct(cotangent.shape, BF16),
            jax.ShapeDtypeStruct(memory.shape, BF16),
        ),
        in_specs=[pl.BlockSpec(memory_space=pl.ANY)] * 7,
        out_specs=(pl.BlockSpec(memory_space=pltpu.VMEM),) * 3,
        scratch_shapes=scratch,
        compiler_params=pltpu.CompilerParams(
            collective_id=0, has_side_effects=True, vmem_limit_bytes=62 * 2**20
        ),
        cost_estimate=pl.CostEstimate(flops=23 * 10**9, bytes_accessed=18 * 2**20, transcendentals=2**19),
    )(tokens, cotangent, memory, w_query, w_key, w_value, w_out)
    return pl.pallas_call(
        hand_over,
        out_shape=tuple(jax.ShapeDtypeStruct(r.shape, r.dtype) for r in results),
        in_specs=[pl.BlockSpec(memory_space=pltpu.VMEM)] * 3,
        out_specs=(pl.BlockSpec(memory_space=pltpu.VMEM),) * 3,
    )(*results)


def solution(mesh):
    placed = (
        P("section", None, "tp"),
        P("section", None, "tp"),
        P("section", "tp"),
        P("section", None, "tp"),
        P("section", None, "tp"),
        P("section", None, "tp"),
        P("section", "tp", None),
    )
    return jax.shard_map(
        on_device,
        mesh=mesh,
        in_specs=placed,
        out_specs=(P("section", None, "tp"), P("section", None, "tp"), P("section", "tp")),
        check_vma=False,
    )
```

```python
import functools

import jax
import jax.numpy as jnp
from jax import lax
from jax.experimental import pallas as pl
from jax.experimental.pallas import tpu as pltpu
from jax.sharding import PartitionSpec as P

HEAD_SIZE = 256
HEADS = 2
FEATURES = 512
D = 4096
TARGETS = 256
MEMORY = 1024
OWN_ROWS = 64
SIDE = 2048
SCALE = HEAD_SIZE ** -0.5
BF16 = jnp.bfloat16
F32 = jnp.float32
N_SEMS = 128
N_LOCAL = 48


def dot(a, b):
    return lax.dot_general(a, b, (((1,), (0,)), ((), ())), preferred_element_type=F32)


def dot_nt(a, b):
    return lax.dot_general(a, b, (((1,), (1,)), ((), ())), preferred_element_type=F32)


def dot_tn(a, b):
    return lax.dot_general(a, b, (((0,), (0,)), ((), ())), preferred_element_type=F32)


def aligned(start, size):
    return pl.ds(pl.multiple_of(start, size), size)


def add_rows(dst, srcs):
    rows = dst.shape[0]

    def step(i, _):
        part = aligned(i * 16, 16)
        total = srcs[0][part, :].astype(F32)
        for src in srcs[1:]:
            total = total + src[part, :].astype(F32)
        dst[part, :] = total.astype(dst.dtype)
        return 0

    lax.fori_loop(0, rows // 16, step, 0)


def kernel(
    tokens, cotangent, memory, w_query, w_key, w_value, w_out,
    attended, grad_tokens, grad_memory,
    wkv, wq, wo, mem, tok, cot, kv, gkv, queries_acc, gctx_acc, queries, gctx, ctx, gq, probs, probs_b, dscores,
    core_in, opposite_in, relay_in, final_in, z_in, y_in, att_in, att_z, tgt_in, tgt_z,
    send_sem, recv_sem, local_sem,
):
    section = lax.axis_index("section")
    tp = lax.axis_index("tp")
    c = lax.rem(section, 2)
    x = lax.rem(section // 2, 4)
    y = tp // 2
    zh = lax.rem(tp, 2)
    z = zh * 2 + section // 8

    def device(dx=0, dy=0, dz=0, dc=0):
        to_x, to_y, to_z = lax.rem(x + dx, 4), lax.rem(y + dy, 4), lax.rem(z + dz, 4)
        to_c = lax.rem(c + dc, 2)
        return ((lax.rem(to_z, 2) * 4 + to_x) * 2 + to_c, to_y * 2 + to_z // 2)

    counter = [0, 0]
    sends = []

    def remote(src, dst, where):
        i = counter[0]
        counter[0] += 1
        copy = pltpu.make_async_remote_copy(
            src_ref=src, dst_ref=dst, send_sem=send_sem.at[i], recv_sem=recv_sem.at[i],
            device_id=device(**where), device_id_type=pl.DeviceIdType.MESH,
        )
        copy.start()
        sends.append(copy)
        return copy

    def local(src, dst):
        i = counter[1]
        counter[1] += 1
        copy = pltpu.make_async_copy(src, dst, local_sem.at[i])
        copy.start()
        return copy

    def flush():
        for copy in sends:
            copy.wait_send()
        sends.clear()

    XP, XM, YP, YM = dict(dx=1), dict(dx=3), dict(dy=1), dict(dy=3)
    CORE, ZFAR = dict(dc=1), dict(dz=2)

    def x_at(dx):
        return lax.rem(x + dx, 4)

    def side(high):
        return aligned(high * SIDE, SIDE)

    def piece(dx, core, dz, half=None):
        to_z = lax.rem(z + dz, 4)
        row = core * 128 + lax.rem(to_z, 2) * 64
        rows = aligned(row, 64) if half is None else aligned(row + half * 32, 32)
        return mem.at[x_at(dx), rows, side(to_z // 2)]

    def block(buf, high, dy):
        return buf.at[:, aligned(high * SIDE + lax.rem(y + dy, 4) * FEATURES, FEATURES)]

    own_mem = mem.at[x, aligned(c * 128 + lax.rem(z, 2) * 64, 64), aligned(zh * SIDE + y * FEATURES, FEATURES)]
    near, far = zh, 1 - zh

    mem_load = local(memory, own_mem)
    tok_load = local(tokens.at[0], block(tok, near, 0))
    cot_load = local(cotangent.at[0], block(cot, near, 0))
    barrier = pltpu.get_barrier_semaphore()
    peers = [XP, XM, YP, YM, dict(dy=2), dict(dz=1), dict(dz=3), ZFAR, CORE]
    for where in peers:
        pl.semaphore_signal(barrier, inc=1, device_id=device(**where), device_id_type=pl.DeviceIdType.MESH)
    pl.semaphore_wait(barrier, len(peers))

    mem_y = {dy: remote(memory, own_mem, dict(dy=dy)) for dy in (1, 3, 2)}
    right, left, core_own, mem_z = {}, {}, {}, {}
    right[0] = [remote(memory, own_mem, XP)]
    left[0] = [remote(memory, own_mem, XM)]
    mem_z[1] = [remote(memory, own_mem, dict(dz=1))]
    mem_z[3] = [remote(memory, own_mem, dict(dz=3))]
    tok_z = remote(tokens.at[0], block(tok, near, 0), ZFAR)
    mem_load.wait()
    for dy in (1, 3, 2):
        mem_y[dy].wait_recv()
        here = mem.at[
            x, aligned(c * 128 + lax.rem(z, 2) * 64, 64), aligned(zh * SIDE + lax.rem(y + 4 - dy, 4) * FEATURES, FEATURES)
        ]
        right[0].append(remote(here, here, XP))
        left[0].append(remote(here, here, XM))
        mem_z[1].append(remote(here, here, dict(dz=1)))
        mem_z[3].append(remote(here, here, dict(dz=3)))
    own = piece(0, c, 0)
    core_right, core_left, core_opposite = {}, {}, {}
    on_right, on_left = {}, {}

    def spread(dz):
        here = piece(0, c, dz)
        right[dz] = [remote(here, here, XP)]
        left[dz] = [remote(here, here, XM)]
        core_own[dz] = remote(here, here, CORE)

    def spread_targets():
        t, g = tokens.at[0], cotangent.at[0]
        t_dst, g_dst = block(tok, near, 0), block(cot, near, 0)
        t_right = remote(t, t_dst, YP)
        g_left = remote(g, g_dst, YM)
        g_right = remote(g, g_dst, YP)
        t_left = remote(t, t_dst, YM)
        return t_right, g_left, g_right, t_left

    def spread_far(buf):
        here = block(buf, far, 0)
        return remote(here, here, YP), remote(here, here, YM)

    def arrive_x(dz):
        for copy in right[dz]:
            copy.wait_recv()
        if dz == 0:
            on_right[dz] = remote(piece(3, c, dz, 0), piece(3, c, dz, 0), XP)
        core_left[dz] = remote(piece(3, c, dz), piece(3, c, dz), CORE)
        for copy in left[dz]:
            copy.wait_recv()
        if dz == 0:
            on_left[dz] = remote(piece(1, c, dz, 1), piece(1, c, dz, 1), XM)
        core_right[dz] = remote(piece(1, c, dz), piece(1, c, dz), CORE)

    def arrive_opposite(dz):
        on_right[dz].wait_recv()
        a = remote(piece(2, c, dz, 0), piece(2, c, dz, 0), CORE)
        on_left[dz].wait_recv()
        b = remote(piece(2, c, dz, 1), piece(2, c, dz, 1), CORE)
        core_opposite[dz] = (a, b)

    def arrive_opposite_z(dz):
        opposite_z[4 - dz].wait_recv()
        core_opposite[dz] = (remote(piece(2, c, dz), piece(2, c, dz), CORE),)

    def forward_targets(high, ring):
        t_right, g_left, g_right, t_left = ring
        t_right.wait_recv()
        t_on = remote(block(tok, high, 3), block(tok, high, 3), YP)
        g_left.wait_recv()
        g_on = remote(block(cot, high, 1), block(cot, high, 1), YM)
        return t_on, g_on

    def keys_values(dx):
        to_x = x_at(dx)
        rows = aligned(to_x * 256, 256)

        def step(n, _):
            cols = aligned(n * 512, 512)
            kv[rows, cols] = dot(mem[to_x], wkv[:, cols]).astype(BF16)
            return 0

        lax.fori_loop(0, 2, step, 0)

    core_own[0] = remote(own, own, CORE)
    near_ring = spread_targets()
    kv_loads, q_loads, o_loads = [], [], []
    for high in range(2):
        for row in range(4):
            src = pl.ds((row * 2 + high) * FEATURES, FEATURES)
            dst = pl.ds(high * SIDE + row * FEATURES, FEATURES)
            kv_loads.append(local(w_key.at[0, src, :], wkv.at[dst, pl.ds(0, FEATURES)]))
            kv_loads.append(local(w_value.at[0, src, :], wkv.at[dst, pl.ds(FEATURES, FEATURES)]))
    tok_z.wait_recv()
    far_tok = spread_far(tok)
    arrive_x(0)
    for dz in (1, 3):
        for copy in mem_z[4 - dz]:
            copy.wait_recv()
        spread(dz)
    mem_z[2] = remote(own, own, ZFAR)
    cot_z = remote(cotangent.at[0], block(cot, near, 0), ZFAR)
    for high in range(2):
        for row in range(4):
            src = pl.ds((row * 2 + high) * FEATURES, FEATURES)
            dst = pl.ds(high * SIDE + row * FEATURES, FEATURES)
            q_loads.append(local(w_query.at[0, src, :], wq.at[dst, :]))
            o_loads.append(local(w_out.at[0, :, src], wo.at[:, dst]))

    near_on = forward_targets(near, near_ring)
    arrive_opposite(0)
    opposite_z = {dz: remote(piece(2, c, 0), piece(2, c, 0), dict(dz=dz)) for dz in (1, 3, 2)}
    mem_z[2].wait_recv()
    spread(2)
    cot_z.wait_recv()
    far_cot = spread_far(cot)
    for copy in kv_loads:
        copy.wait()
    for dz in (0, 1, 3, 2):
        core_own[dz].wait_recv()
    keys_values(0)
    arrive_x(1)
    arrive_x(3)
    far_tok[0].wait_recv()
    far_t_on = remote(block(tok, far, 3), block(tok, far, 3), YP)

    def complete(ring, on):
        t_right, g_left, g_right, t_left = ring
        g_right.wait_recv()
        t_left.wait_recv()
        on[0].wait_recv()
        on[1].wait_recv()

    complete(near_ring, near_on)
    tok_load.wait()
    cot_load.wait()
    for copy in q_loads:
        copy.wait()
    for copy in o_loads:
        copy.wait()

    def project_near():
        queries_acc[...] = dot(tok[:, side(near)], wq[side(near), :])
        gctx_acc[...] = dot_nt(cot[:, side(near)], wo[:, side(near)])

    project_near()
    arrive_opposite_z(1)
    arrive_opposite_z(3)
    arrive_x(2)
    far_cot[1].wait_recv()
    far_g_on = remote(block(cot, far, 1), block(cot, far, 1), YM)
    far_on = (far_t_on, far_g_on)
    far_ring = (far_tok[0], far_cot[1], far_cot[0], far_tok[1])
    arrive_opposite_z(2)
    for dz in (0, 1, 3, 2):
        core_right[dz].wait_recv()
    keys_values(1)
    for dz in (0, 1, 3, 2):
        core_left[dz].wait_recv()
    keys_values(3)
    for dz in (0, 1, 3, 2):
        for copy in core_opposite[dz]:
            copy.wait_recv()
    keys_values(2)
    complete(far_ring, far_on)

    def project_far():
        queries[...] = (queries_acc[...] + dot(tok[:, side(far)], wq[side(far), :])).astype(BF16)
        gctx[...] = (gctx_acc[...] + dot_nt(cot[:, side(far)], wo[:, side(far)])).astype(BF16)

    project_far()
    flush()

    for h in range(HEADS):
        k_cols = pl.ds(h * HEAD_SIZE, HEAD_SIZE)
        v_cols = pl.ds(FEATURES + h * HEAD_SIZE, HEAD_SIZE)
        scores = dot_nt(queries[:, k_cols], kv[:, k_cols]) * SCALE
        top = jnp.max(scores, axis=-1, keepdims=True)
        weights = jnp.exp(scores - top)
        p = weights / jnp.sum(weights, axis=-1, keepdims=True)
        probs[...] = p
        p_b = p.astype(BF16)
        probs_b[h] = p_b
        grad_probs = dot_nt(gctx[:, k_cols], kv[:, v_cols])
        p = probs[...]
        delta = jnp.sum(grad_probs * p, axis=-1, keepdims=True)
        ds = (p * (grad_probs - delta) * SCALE).astype(BF16)
        dscores[h] = ds
        gkv[:, k_cols] = dot_tn(ds, queries[:, k_cols]).astype(BF16)
        gkv[:, v_cols] = dot_tn(probs_b[h], gctx[:, k_cols]).astype(BF16)

    def memory_terms(dx, high):
        to_x = x_at(dx)
        rows = aligned(to_x * 256, 256)

        def step(n, _):
            cols = aligned(high * SIDE + n * 512, 512)
            mem[to_x, :, cols] = dot_nt(gkv[rows, :], wkv[cols, :]).astype(BF16)
            return 0

        lax.fori_loop(0, 4, step, 0)
        return remote(
            mem.at[to_x, aligned((1 - c) * 128, 128), side(high)], core_in.at[to_x, :, side(high)], CORE
        )

    zl = lax.rem(z, 2)

    def part(dx, high, low):
        return mem.at[x_at(dx), aligned(c * 128 + low * 64, 64), side(high)]

    def pair_sum(dx, high, low, extra=()):
        here = part(dx, high, low)
        other = core_in.at[x_at(dx), aligned(low * 64, 64), side(high)]
        add_rows(here, [here, other] + list(extra))
        return here

    def far_relay(buf, inbox):
        return remote(block(buf, far, 2), inbox.at[0], YP)

    def near_relay(buf, inbox):
        return remote(block(buf, near, 2), inbox.at[1], YM)

    def far_on_left(buf, inbox, terms):
        terms(far, 3)
        return remote(block(buf, far, 3), inbox.at[3], YM)

    def near_on_right(buf, inbox, terms):
        terms(near, 1)
        return remote(block(buf, near, 1), inbox.at[2], YP)

    def far_on_right(buf, inbox, a_relay):
        a_relay.wait_recv()
        here = block(buf, far, 1)
        add_rows(here, [here, inbox.at[0]])
        return remote(here, inbox.at[4], YP)

    def near_on_left(buf, inbox, b_relay):
        b_relay.wait_recv()
        here = block(buf, near, 3)
        add_rows(here, [here, inbox.at[1]])
        return remote(here, inbox.at[5], YM)

    def ring_far(buf, inbox, z_box, a_left, a_right):
        a_left.wait_recv()
        a_right.wait_recv()
        here = block(buf, far, 0)
        add_rows(here, [here, inbox.at[3], inbox.at[4]])
        return remote(here, z_box, ZFAR)

    def ring_near(buf, inbox, z_box, b_right, b_left, z_copy, out):
        b_right.wait_recv()
        b_left.wait_recv()
        z_copy.wait_recv()
        add_rows(out.at[0], [block(buf, near, 0), inbox.at[2], inbox.at[5], z_box])

    def out_terms(high, dy):
        cols = aligned(high * SIDE + lax.rem(y + dy, 4) * FEATURES, FEATURES)
        tok[:, cols] = dot(ctx[...], wo[:, cols]).astype(BF16)

    def target_terms(high, dy):
        rows = aligned(high * SIDE + lax.rem(y + dy, 4) * FEATURES, FEATURES)
        cot[:, rows] = dot_nt(gq[...], wq[rows, :]).astype(BF16)

    lows = (zl, 1 - zl)
    far_lows, near_lows = lows, lows[::-1]

    def x_final_far(i):
        far_left[i].wait_recv()
        far_right[i].wait_recv()
        here = pair_sum(0, far, far_lows[i], [final_in.at[0, i], final_in.at[1, i]])
        if i == 0:
            return remote(here, z_in.at[0], ZFAR)
        return remote(here, z_in.at[1], dict(dz=3 - 2 * zl))

    def x_final_near(i):
        near_right[i].wait_recv()
        near_left[i].wait_recv()
        here = pair_sum(0, near, near_lows[i], [final_in.at[0, 2 + i], final_in.at[1, 2 + i]])
        if i == 0:
            return remote(here, z_in.at[2], dict(dz=1 + 2 * zl))
        return here

    def half(dx, i):
        return mem.at[x_at(dx), aligned(c * 128 + zl * 64 + i * 32, 32), side(near)]

    core_1f = memory_terms(1, far)
    core_3f = memory_terms(3, far)
    for h in range(HEADS):
        cols = pl.ds(h * HEAD_SIZE, HEAD_SIZE)
        v_cols = pl.ds(FEATURES + h * HEAD_SIZE, HEAD_SIZE)
        ctx[:, cols] = dot(probs_b[h], kv[:, v_cols]).astype(BF16)
    out_terms(far, 2)
    att_far_relay = far_relay(tok, att_in)
    att_far_left = far_on_left(tok, att_in, out_terms)
    core_1f.wait_recv()
    far_right = [remote(pair_sum(1, far, zl), final_in.at[0, 0], XP)]
    core_3f.wait_recv()
    far_left = [remote(pair_sum(3, far, zl), final_in.at[1, 0], XM)]
    core_2f = memory_terms(2, far)
    core_2n = memory_terms(2, near)
    for h in range(HEADS):
        cols = pl.ds(h * HEAD_SIZE, HEAD_SIZE)
        gq[:, cols] = dot(dscores[h], kv[:, cols]).astype(BF16)
    core_2f.wait_recv()
    opposite_other = remote(pair_sum(2, far, 1 - zl), opposite_in.at[1], dict(dz=3 - 2 * zl))
    opposite_same = remote(pair_sum(2, far, zl), opposite_in.at[2], ZFAR)
    core_2n.wait_recv()
    opposite_near = remote(pair_sum(2, near, 1 - zl), opposite_in.at[0], dict(dz=1 + 2 * zl))
    far_right.append(remote(pair_sum(1, far, 1 - zl), final_in.at[0, 1], XP))
    far_left.append(remote(pair_sum(3, far, 1 - zl), final_in.at[1, 1], XM))
    out_terms(far, 1)
    core_0f = memory_terms(0, far)
    target_terms(far, 2)
    target_terms(far, 1)
    out_terms(near, 2)
    att_far_right = far_on_right(tok, att_in, att_far_relay)
    tgt_far_relay = far_relay(cot, tgt_in)
    tgt_far_left = far_on_left(cot, tgt_in, target_terms)
    core_0f.wait_recv()
    z_far0 = x_final_far(0)
    core_1n = memory_terms(1, near)
    att_near_relay = near_relay(tok, att_in)
    core_3n = memory_terms(3, near)
    core_1n.wait_recv()
    near_right = [remote(pair_sum(1, near, 1 - zl), final_in.at[0, 2], XP)]
    core_3n.wait_recv()
    near_left = [remote(pair_sum(3, near, 1 - zl), final_in.at[1, 2], XM)]
    out_terms(far, 0)
    target_terms(near, 2)
    z_far1 = x_final_far(1)
    att_far = ring_far(tok, att_in, att_z, att_far_left, att_far_right)
    tgt_near_relay = near_relay(cot, tgt_in)
    for copy in (opposite_near, opposite_other, opposite_same):
        copy.wait_recv()
    pair_sum(2, near, zl, [opposite_in.at[0], opposite_in.at[1], opposite_in.at[2]])
    relay_right = remote(half(2, 0), relay_in.at[0], XP)
    relay_left = remote(half(2, 1), relay_in.at[1], XM)
    att_near_right = near_on_right(tok, att_in, out_terms)
    target_terms(far, 0)
    out_terms(near, 3)
    target_terms(near, 3)
    pair_sum(1, near, zl)
    pair_sum(3, near, zl)
    tgt_far_right = far_on_right(cot, tgt_in, tgt_far_relay)
    relay_right.wait_recv()
    add_rows(half(1, 0), [half(1, 0), relay_in.at[0]])
    near_right.append(remote(part(1, near, zl), final_in.at[0, 3], XP))
    relay_left.wait_recv()
    add_rows(half(3, 1), [half(3, 1), relay_in.at[1]])
    near_left.append(remote(part(3, near, zl), final_in.at[1, 3], XM))
    tgt_near_right = near_on_right(cot, tgt_in, target_terms)
    att_near_left = near_on_left(tok, att_in, att_near_relay)
    core_0n = memory_terms(0, near)
    out_terms(near, 0)
    target_terms(near, 0)
    core_0n.wait_recv()
    z_near0 = x_final_near(0)
    tgt_near_left = near_on_left(cot, tgt_in, tgt_near_relay)
    tgt_far = ring_far(cot, tgt_in, tgt_z, tgt_far_left, tgt_far_right)
    here = x_final_near(1)
    for copy in (z_far0, z_near0, z_far1):
        copy.wait_recv()
    add_rows(here, [here, z_in.at[0], z_in.at[1], z_in.at[2]])

    def y_part(dy):
        return mem.at[
            x, aligned(c * 128 + zl * 64, 64), aligned(zh * SIDE + lax.rem(y + dy, 4) * FEATURES, FEATURES)
        ]

    y_copies = [remote(y_part(dy), y_in.at[dy - 1], dict(dy=dy)) for dy in (2, 1, 3)]
    ring_near(tok, att_in, att_z, att_near_right, att_near_left, att_far, attended)
    ring_near(cot, tgt_in, tgt_z, tgt_near_right, tgt_near_left, tgt_far, grad_tokens)
    for copy in y_copies:
        copy.wait_recv()
    add_rows(grad_memory, [y_part(0), y_in.at[0], y_in.at[1], y_in.at[2]])
    flush()


def hand_over(a_in, b_in, c_in, a_out, b_out, c_out):
    a_out[...] = a_in[...]
    b_out[...] = b_in[...]
    c_out[...] = c_in[...]


def on_device(tokens, cotangent, memory, w_query, w_key, w_value, w_out):
    vmem = pltpu.VMEM
    scratch = [
        vmem((D, 2 * FEATURES), BF16),
        vmem((D, FEATURES), BF16),
        vmem((FEATURES, D), BF16),
        vmem((4, 256, D), BF16),
        vmem((TARGETS, D), BF16),
        vmem((TARGETS, D), BF16),
        vmem((MEMORY, 2 * FEATURES), BF16),
        vmem((MEMORY, 2 * FEATURES), BF16),
        vmem((TARGETS, FEATURES), F32),
        vmem((TARGETS, FEATURES), F32),
        vmem((TARGETS, FEATURES), BF16),
        vmem((TARGETS, FEATURES), BF16),
        vmem((TARGETS, FEATURES), BF16),
        vmem((TARGETS, FEATURES), BF16),
        vmem((TARGETS, MEMORY), F32),
        vmem((HEADS, TARGETS, MEMORY), BF16),
        vmem((HEADS, TARGETS, MEMORY), BF16),
        vmem((4, 128, D), BF16),
        vmem((3, OWN_ROWS, SIDE), BF16),
        vmem((2, OWN_ROWS // 2, SIDE), BF16),
        vmem((2, 4, OWN_ROWS, SIDE), BF16),
        vmem((3, OWN_ROWS, SIDE), BF16),
        vmem((3, OWN_ROWS, FEATURES), BF16),
        vmem((6, TARGETS, FEATURES), BF16),
        vmem((TARGETS, FEATURES), BF16),
        vmem((6, TARGETS, FEATURES), BF16),
        vmem((TARGETS, FEATURES), BF16),
        pltpu.SemaphoreType.DMA((N_SEMS,)),
        pltpu.SemaphoreType.DMA((N_SEMS,)),
        pltpu.SemaphoreType.DMA((N_LOCAL,)),
    ]
    results = pl.pallas_call(
        kernel,
        out_shape=(
            jax.ShapeDtypeStruct(tokens.shape, BF16),
            jax.ShapeDtypeStruct(cotangent.shape, BF16),
            jax.ShapeDtypeStruct(memory.shape, BF16),
        ),
        in_specs=[pl.BlockSpec(memory_space=pl.ANY)] * 7,
        out_specs=(pl.BlockSpec(memory_space=pltpu.VMEM),) * 3,
        scratch_shapes=scratch,
        compiler_params=pltpu.CompilerParams(
            collective_id=0, has_side_effects=True, vmem_limit_bytes=62 * 2**20
        ),
        cost_estimate=pl.CostEstimate(flops=23 * 10**9, bytes_accessed=18 * 2**20, transcendentals=2**19),
    )(tokens, cotangent, memory, w_query, w_key, w_value, w_out)
    return pl.pallas_call(
        hand_over,
        out_shape=tuple(jax.ShapeDtypeStruct(r.shape, r.dtype) for r in results),
        in_specs=[pl.BlockSpec(memory_space=pltpu.VMEM)] * 3,
        out_specs=(pl.BlockSpec(memory_space=pltpu.VMEM),) * 3,
    )(*results)


def solution(mesh):
    placed = (
        P("section", None, "tp"),
        P("section", None, "tp"),
        P("section", "tp"),
        P("section", None, "tp"),
        P("section", None, "tp"),
        P("section", None, "tp"),
        P("section", "tp", None),
    )
    return jax.shard_map(
        on_device,
        mesh=mesh,
        in_specs=placed,
        out_specs=(P("section", None, "tp"), P("section", None, "tp"), P("section", "tp")),
        check_vma=False,
    )
```

```python
import functools

import jax
import jax.numpy as jnp
from jax import lax
from jax.experimental import pallas as pl
from jax.experimental.pallas import tpu as pltpu
from jax.sharding import PartitionSpec as P

HEAD_SIZE = 256
HEADS = 2
FEATURES = 512
D = 4096
TARGETS = 256
MEMORY = 1024
OWN_ROWS = 64
SIDE = 2048
SCALE = HEAD_SIZE ** -0.5
BF16 = jnp.bfloat16
F32 = jnp.float32
N_SEMS = 128
N_LOCAL = 48


def dot(a, b):
    return lax.dot_general(a, b, (((1,), (0,)), ((), ())), preferred_element_type=F32)


def dot_nt(a, b):
    return lax.dot_general(a, b, (((1,), (1,)), ((), ())), preferred_element_type=F32)


def dot_tn(a, b):
    return lax.dot_general(a, b, (((0,), (0,)), ((), ())), preferred_element_type=F32)


def aligned(start, size):
    return pl.ds(pl.multiple_of(start, size), size)


def add_rows(dst, srcs):
    rows = dst.shape[0]

    def step(i, _):
        part = aligned(i * 16, 16)
        total = srcs[0][part, :].astype(F32)
        for src in srcs[1:]:
            total = total + src[part, :].astype(F32)
        dst[part, :] = total.astype(dst.dtype)
        return 0

    lax.fori_loop(0, rows // 16, step, 0)


def kernel(
    tokens, cotangent, memory, w_query, w_key, w_value, w_out,
    attended, grad_tokens, grad_memory,
    wkv, wq, wo, mem, tok, cot, kv, gkv, queries_acc, gctx_acc, queries, gctx, ctx, gq, probs, probs_b, dscores,
    core_in, opposite_in, relay_in, final_in, z_in, y_in, att_in, att_z, tgt_in, tgt_z,
    send_sem, recv_sem, local_sem,
):
    section = lax.axis_index("section")
    tp = lax.axis_index("tp")
    c = lax.rem(section, 2)
    x = lax.rem(section // 2, 4)
    y = tp // 2
    zh = lax.rem(tp, 2)
    z = zh * 2 + section // 8

    def device(dx=0, dy=0, dz=0, dc=0):
        to_x, to_y, to_z = lax.rem(x + dx, 4), lax.rem(y + dy, 4), lax.rem(z + dz, 4)
        to_c = lax.rem(c + dc, 2)
        return ((lax.rem(to_z, 2) * 4 + to_x) * 2 + to_c, to_y * 2 + to_z // 2)

    counter = [0, 0]
    sends = []

    def remote(src, dst, where):
        i = counter[0]
        counter[0] += 1
        copy = pltpu.make_async_remote_copy(
            src_ref=src, dst_ref=dst, send_sem=send_sem.at[i], recv_sem=recv_sem.at[i],
            device_id=device(**where), device_id_type=pl.DeviceIdType.MESH,
        )
        copy.start()
        sends.append(copy)
        return copy

    def local(src, dst):
        i = counter[1]
        counter[1] += 1
        copy = pltpu.make_async_copy(src, dst, local_sem.at[i])
        copy.start()
        return copy

    def flush():
        for copy in sends:
            copy.wait_send()
        sends.clear()

    XP, XM, YP, YM = dict(dx=1), dict(dx=3), dict(dy=1), dict(dy=3)
    CORE, ZFAR = dict(dc=1), dict(dz=2)

    def x_at(dx):
        return lax.rem(x + dx, 4)

    def side(high):
        return aligned(high * SIDE, SIDE)

    def piece(dx, core, dz, half=None):
        to_z = lax.rem(z + dz, 4)
        row = core * 128 + lax.rem(to_z, 2) * 64
        rows = aligned(row, 64) if half is None else aligned(row + half * 32, 32)
        return mem.at[x_at(dx), rows, side(to_z // 2)]

    def block(buf, high, dy):
        return buf.at[:, aligned(high * SIDE + lax.rem(y + dy, 4) * FEATURES, FEATURES)]

    own_mem = mem.at[x, aligned(c * 128 + lax.rem(z, 2) * 64, 64), aligned(zh * SIDE + y * FEATURES, FEATURES)]
    near, far = zh, 1 - zh

    mem_load = local(memory, own_mem)
    tok_load = local(tokens.at[0], block(tok, near, 0))
    cot_load = local(cotangent.at[0], block(cot, near, 0))
    barrier = pltpu.get_barrier_semaphore()
    peers = [XP, XM, YP, YM, dict(dy=2), dict(dz=1), dict(dz=3), ZFAR, CORE]
    for where in peers:
        pl.semaphore_signal(barrier, inc=1, device_id=device(**where), device_id_type=pl.DeviceIdType.MESH)
    pl.semaphore_wait(barrier, len(peers))

    mem_y = {dy: remote(memory, own_mem, dict(dy=dy)) for dy in (1, 3, 2)}
    right, left, core_own, mem_z = {}, {}, {}, {}
    right[0] = [remote(memory, own_mem, XP)]
    left[0] = [remote(memory, own_mem, XM)]
    mem_z[1] = [remote(memory, own_mem, dict(dz=1))]
    mem_z[3] = [remote(memory, own_mem, dict(dz=3))]
    tok_z = remote(tokens.at[0], block(tok, near, 0), ZFAR)
    mem_load.wait()
    for dy in (1, 3, 2):
        mem_y[dy].wait_recv()
        here = mem.at[
            x, aligned(c * 128 + lax.rem(z, 2) * 64, 64), aligned(zh * SIDE + lax.rem(y + 4 - dy, 4) * FEATURES, FEATURES)
        ]
        right[0].append(remote(here, here, XP))
        left[0].append(remote(here, here, XM))
        mem_z[1].append(remote(here, here, dict(dz=1)))
        mem_z[3].append(remote(here, here, dict(dz=3)))
    own = piece(0, c, 0)
    core_right, core_left, core_opposite = {}, {}, {}
    on_right, on_left = {}, {}

    def spread(dz):
        here = piece(0, c, dz)
        right[dz] = [remote(here, here, XP)]
        left[dz] = [remote(here, here, XM)]
        core_own[dz] = remote(here, here, CORE)

    def spread_targets():
        t, g = tokens.at[0], cotangent.at[0]
        t_dst, g_dst = block(tok, near, 0), block(cot, near, 0)
        t_right = remote(t, t_dst, YP)
        g_left = remote(g, g_dst, YM)
        g_right = remote(g, g_dst, YP)
        t_left = remote(t, t_dst, YM)
        return t_right, g_left, g_right, t_left

    def spread_far(buf):
        here = block(buf, far, 0)
        return remote(here, here, YP), remote(here, here, YM)

    def arrive_x(dz):
        for copy in right[dz]:
            copy.wait_recv()
        if dz in (0, 2):
            on_right[dz] = remote(piece(3, c, dz, 0), piece(3, c, dz, 0), XP)
        core_left[dz] = remote(piece(3, c, dz), piece(3, c, dz), CORE)
        for copy in left[dz]:
            copy.wait_recv()
        if dz in (0, 2):
            on_left[dz] = remote(piece(1, c, dz, 1), piece(1, c, dz, 1), XM)
        core_right[dz] = remote(piece(1, c, dz), piece(1, c, dz), CORE)

    def arrive_opposite(dz):
        on_right[dz].wait_recv()
        a = remote(piece(2, c, dz, 0), piece(2, c, dz, 0), CORE)
        on_left[dz].wait_recv()
        b = remote(piece(2, c, dz, 1), piece(2, c, dz, 1), CORE)
        core_opposite[dz] = (a, b)

    def arrive_opposite_z(dz):
        opposite_z[4 - dz].wait_recv()
        core_opposite[dz] = (remote(piece(2, c, dz), piece(2, c, dz), CORE),)

    def forward_targets(high, ring):
        t_right, g_left, g_right, t_left = ring
        t_right.wait_recv()
        t_on = remote(block(tok, high, 3), block(tok, high, 3), YP)
        g_left.wait_recv()
        g_on = remote(block(cot, high, 1), block(cot, high, 1), YM)
        return t_on, g_on

    def keys_values(dx):
        to_x = x_at(dx)
        rows = aligned(to_x * 256, 256)

        def step(n, _):
            cols = aligned(n * 512, 512)
            kv[rows, cols] = dot(mem[to_x], wkv[:, cols]).astype(BF16)
            return 0

        lax.fori_loop(0, 2, step, 0)

    core_own[0] = remote(own, own, CORE)
    near_ring = spread_targets()
    kv_loads, q_loads, o_loads = [], [], []
    for high in range(2):
        for row in range(4):
            src = pl.ds((row * 2 + high) * FEATURES, FEATURES)
            dst = pl.ds(high * SIDE + row * FEATURES, FEATURES)
            kv_loads.append(local(w_key.at[0, src, :], wkv.at[dst, pl.ds(0, FEATURES)]))
            kv_loads.append(local(w_value.at[0, src, :], wkv.at[dst, pl.ds(FEATURES, FEATURES)]))
    tok_z.wait_recv()
    far_tok = spread_far(tok)
    arrive_x(0)
    for dz in (1, 3):
        for copy in mem_z[4 - dz]:
            copy.wait_recv()
        spread(dz)
    mem_z[2] = remote(own, own, ZFAR)
    cot_z = remote(cotangent.at[0], block(cot, near, 0), ZFAR)
    for high in range(2):
        for row in range(4):
            src = pl.ds((row * 2 + high) * FEATURES, FEATURES)
            dst = pl.ds(high * SIDE + row * FEATURES, FEATURES)
            q_loads.append(local(w_query.at[0, src, :], wq.at[dst, :]))
            o_loads.append(local(w_out.at[0, :, src], wo.at[:, dst]))

    near_on = forward_targets(near, near_ring)
    arrive_opposite(0)
    opposite_z = {dz: remote(piece(2, c, 0), piece(2, c, 0), dict(dz=dz)) for dz in (1, 3)}
    mem_z[2].wait_recv()
    spread(2)
    cot_z.wait_recv()
    far_cot = spread_far(cot)
    for copy in kv_loads:
        copy.wait()
    for dz in (0, 1, 3, 2):
        core_own[dz].wait_recv()
    keys_values(0)
    arrive_x(1)
    arrive_x(3)
    far_tok[0].wait_recv()
    far_t_on = remote(block(tok, far, 3), block(tok, far, 3), YP)

    def complete(ring, on):
        t_right, g_left, g_right, t_left = ring
        g_right.wait_recv()
        t_left.wait_recv()
        on[0].wait_recv()
        on[1].wait_recv()

    complete(near_ring, near_on)
    tok_load.wait()
    cot_load.wait()
    for copy in q_loads:
        copy.wait()
    for copy in o_loads:
        copy.wait()

    def project_near():
        queries_acc[...] = dot(tok[:, side(near)], wq[side(near), :])
        gctx_acc[...] = dot_nt(cot[:, side(near)], wo[:, side(near)])

    project_near()
    arrive_opposite_z(1)
    arrive_opposite_z(3)
    arrive_x(2)
    far_cot[1].wait_recv()
    far_g_on = remote(block(cot, far, 1), block(cot, far, 1), YM)
    far_on = (far_t_on, far_g_on)
    far_ring = (far_tok[0], far_cot[1], far_cot[0], far_tok[1])
    for dz in (0, 1, 3, 2):
        core_right[dz].wait_recv()
    keys_values(1)
    arrive_opposite(2)
    for dz in (0, 1, 3, 2):
        core_left[dz].wait_recv()
    keys_values(3)
    for dz in (0, 1, 3, 2):
        for copy in core_opposite[dz]:
            copy.wait_recv()
    keys_values(2)
    complete(far_ring, far_on)

    def project_far():
        queries[...] = (queries_acc[...] + dot(tok[:, side(far)], wq[side(far), :])).astype(BF16)
        gctx[...] = (gctx_acc[...] + dot_nt(cot[:, side(far)], wo[:, side(far)])).astype(BF16)

    project_far()
    flush()

    for h in range(HEADS):
        k_cols = pl.ds(h * HEAD_SIZE, HEAD_SIZE)
        v_cols = pl.ds(FEATURES + h * HEAD_SIZE, HEAD_SIZE)
        scores = dot_nt(queries[:, k_cols], kv[:, k_cols]) * SCALE
        top = jnp.max(scores, axis=-1, keepdims=True)
        weights = jnp.exp(scores - top)
        p = weights / jnp.sum(weights, axis=-1, keepdims=True)
        probs[...] = p
        p_b = p.astype(BF16)
        probs_b[h] = p_b
        grad_probs = dot_nt(gctx[:, k_cols], kv[:, v_cols])
        p = probs[...]
        delta = jnp.sum(grad_probs * p, axis=-1, keepdims=True)
        ds = (p * (grad_probs - delta) * SCALE).astype(BF16)
        dscores[h] = ds
        gkv[:, k_cols] = dot_tn(ds, queries[:, k_cols]).astype(BF16)
        gkv[:, v_cols] = dot_tn(probs_b[h], gctx[:, k_cols]).astype(BF16)

    def memory_terms(dx, high):
        to_x = x_at(dx)
        rows = aligned(to_x * 256, 256)

        def step(n, _):
            cols = aligned(high * SIDE + n * 512, 512)
            mem[to_x, :, cols] = dot_nt(gkv[rows, :], wkv[cols, :]).astype(BF16)
            return 0

        lax.fori_loop(0, 4, step, 0)
        return remote(
            mem.at[to_x, aligned((1 - c) * 128, 128), side(high)], core_in.at[to_x, :, side(high)], CORE
        )

    zl = lax.rem(z, 2)

    def part(dx, high, low):
        return mem.at[x_at(dx), aligned(c * 128 + low * 64, 64), side(high)]

    def pair_sum(dx, high, low, extra=()):
        here = part(dx, high, low)
        other = core_in.at[x_at(dx), aligned(low * 64, 64), side(high)]
        add_rows(here, [here, other] + list(extra))
        return here

    def far_relay(buf, inbox):
        return remote(block(buf, far, 2), inbox.at[0], YP)

    def near_relay(buf, inbox):
        return remote(block(buf, near, 2), inbox.at[1], YM)

    def far_on_left(buf, inbox, terms):
        terms(far, 3)
        return remote(block(buf, far, 3), inbox.at[3], YM)

    def near_on_right(buf, inbox, terms):
        terms(near, 1)
        return remote(block(buf, near, 1), inbox.at[2], YP)

    def far_on_right(buf, inbox, a_relay):
        a_relay.wait_recv()
        here = block(buf, far, 1)
        add_rows(here, [here, inbox.at[0]])
        return remote(here, inbox.at[4], YP)

    def near_on_left(buf, inbox, b_relay):
        b_relay.wait_recv()
        here = block(buf, near, 3)
        add_rows(here, [here, inbox.at[1]])
        return remote(here, inbox.at[5], YM)

    def ring_far(buf, inbox, z_box, a_left, a_right):
        a_left.wait_recv()
        a_right.wait_recv()
        here = block(buf, far, 0)
        add_rows(here, [here, inbox.at[3], inbox.at[4]])
        return remote(here, z_box, ZFAR)

    def ring_near(buf, inbox, z_box, b_right, b_left, z_copy, out):
        b_right.wait_recv()
        b_left.wait_recv()
        z_copy.wait_recv()
        add_rows(out.at[0], [block(buf, near, 0), inbox.at[2], inbox.at[5], z_box])

    def out_terms(high, dy):
        cols = aligned(high * SIDE + lax.rem(y + dy, 4) * FEATURES, FEATURES)
        tok[:, cols] = dot(ctx[...], wo[:, cols]).astype(BF16)

    def target_terms(high, dy):
        rows = aligned(high * SIDE + lax.rem(y + dy, 4) * FEATURES, FEATURES)
        cot[:, rows] = dot_nt(gq[...], wq[rows, :]).astype(BF16)

    lows = (zl, 1 - zl)
    far_lows, near_lows = lows, lows[::-1]

    def x_final_far(i):
        far_left[i].wait_recv()
        far_right[i].wait_recv()
        here = pair_sum(0, far, far_lows[i], [final_in.at[0, i], final_in.at[1, i]])
        if i == 0:
            return remote(here, z_in.at[0], ZFAR)
        return remote(here, z_in.at[1], dict(dz=3 - 2 * zl))

    def x_final_near(i):
        near_right[i].wait_recv()
        near_left[i].wait_recv()
        here = pair_sum(0, near, near_lows[i], [final_in.at[0, 2 + i], final_in.at[1, 2 + i]])
        if i == 0:
            return remote(here, z_in.at[2], dict(dz=1 + 2 * zl))
        return here

    def half(dx, i):
        return mem.at[x_at(dx), aligned(c * 128 + zl * 64 + i * 32, 32), side(near)]

    core_1f = memory_terms(1, far)
    core_3f = memory_terms(3, far)
    for h in range(HEADS):
        cols = pl.ds(h * HEAD_SIZE, HEAD_SIZE)
        v_cols = pl.ds(FEATURES + h * HEAD_SIZE, HEAD_SIZE)
        ctx[:, cols] = dot(probs_b[h], kv[:, v_cols]).astype(BF16)
    out_terms(far, 2)
    att_far_relay = far_relay(tok, att_in)
    att_far_left = far_on_left(tok, att_in, out_terms)
    core_1f.wait_recv()
    far_right = [remote(pair_sum(1, far, zl), final_in.at[0, 0], XP)]
    core_3f.wait_recv()
    far_left = [remote(pair_sum(3, far, zl), final_in.at[1, 0], XM)]
    core_2f = memory_terms(2, far)
    core_2n = memory_terms(2, near)
    for h in range(HEADS):
        cols = pl.ds(h * HEAD_SIZE, HEAD_SIZE)
        gq[:, cols] = dot(dscores[h], kv[:, cols]).astype(BF16)
    core_2f.wait_recv()
    opposite_other = remote(pair_sum(2, far, 1 - zl), opposite_in.at[1], dict(dz=3 - 2 * zl))
    opposite_same = remote(pair_sum(2, far, zl), opposite_in.at[2], ZFAR)
    core_2n.wait_recv()
    opposite_near = remote(pair_sum(2, near, 1 - zl), opposite_in.at[0], dict(dz=1 + 2 * zl))
    far_right.append(remote(pair_sum(1, far, 1 - zl), final_in.at[0, 1], XP))
    far_left.append(remote(pair_sum(3, far, 1 - zl), final_in.at[1, 1], XM))
    out_terms(far, 1)
    core_0f = memory_terms(0, far)
    target_terms(far, 2)
    target_terms(far, 1)
    out_terms(near, 2)
    att_far_right = far_on_right(tok, att_in, att_far_relay)
    tgt_far_relay = far_relay(cot, tgt_in)
    tgt_far_left = far_on_left(cot, tgt_in, target_terms)
    core_0f.wait_recv()
    z_far0 = x_final_far(0)
    core_1n = memory_terms(1, near)
    att_near_relay = near_relay(tok, att_in)
    core_3n = memory_terms(3, near)
    core_1n.wait_recv()
    near_right = [remote(pair_sum(1, near, 1 - zl), final_in.at[0, 2], XP)]
    core_3n.wait_recv()
    near_left = [remote(pair_sum(3, near, 1 - zl), final_in.at[1, 2], XM)]
    out_terms(far, 0)
    target_terms(near, 2)
    z_far1 = x_final_far(1)
    att_far = ring_far(tok, att_in, att_z, att_far_left, att_far_right)
    tgt_near_relay = near_relay(cot, tgt_in)
    for copy in (opposite_near, opposite_other, opposite_same):
        copy.wait_recv()
    pair_sum(2, near, zl, [opposite_in.at[0], opposite_in.at[1], opposite_in.at[2]])
    relay_right = remote(half(2, 0), relay_in.at[0], XP)
    relay_left = remote(half(2, 1), relay_in.at[1], XM)
    att_near_right = near_on_right(tok, att_in, out_terms)
    target_terms(far, 0)
    out_terms(near, 3)
    target_terms(near, 3)
    pair_sum(1, near, zl)
    pair_sum(3, near, zl)
    tgt_far_right = far_on_right(cot, tgt_in, tgt_far_relay)
    relay_right.wait_recv()
    add_rows(half(1, 0), [half(1, 0), relay_in.at[0]])
    near_right.append(remote(part(1, near, zl), final_in.at[0, 3], XP))
    relay_left.wait_recv()
    add_rows(half(3, 1), [half(3, 1), relay_in.at[1]])
    near_left.append(remote(part(3, near, zl), final_in.at[1, 3], XM))
    tgt_near_right = near_on_right(cot, tgt_in, target_terms)
    att_near_left = near_on_left(tok, att_in, att_near_relay)
    core_0n = memory_terms(0, near)
    out_terms(near, 0)
    target_terms(near, 0)
    core_0n.wait_recv()
    z_near0 = x_final_near(0)
    tgt_near_left = near_on_left(cot, tgt_in, tgt_near_relay)
    tgt_far = ring_far(cot, tgt_in, tgt_z, tgt_far_left, tgt_far_right)
    here = x_final_near(1)
    for copy in (z_far0, z_near0, z_far1):
        copy.wait_recv()
    add_rows(here, [here, z_in.at[0], z_in.at[1], z_in.at[2]])

    def y_part(dy):
        return mem.at[
            x, aligned(c * 128 + zl * 64, 64), aligned(zh * SIDE + lax.rem(y + dy, 4) * FEATURES, FEATURES)
        ]

    y_copies = [remote(y_part(dy), y_in.at[dy - 1], dict(dy=dy)) for dy in (2, 1, 3)]
    ring_near(tok, att_in, att_z, att_near_right, att_near_left, att_far, attended)
    ring_near(cot, tgt_in, tgt_z, tgt_near_right, tgt_near_left, tgt_far, grad_tokens)
    for copy in y_copies:
        copy.wait_recv()
    add_rows(grad_memory, [y_part(0), y_in.at[0], y_in.at[1], y_in.at[2]])
    flush()


def hand_over(a_in, b_in, c_in, a_out, b_out, c_out):
    a_out[...] = a_in[...]
    b_out[...] = b_in[...]
    c_out[...] = c_in[...]


def on_device(tokens, cotangent, memory, w_query, w_key, w_value, w_out):
    vmem = pltpu.VMEM
    scratch = [
        vmem((D, 2 * FEATURES), BF16),
        vmem((D, FEATURES), BF16),
        vmem((FEATURES, D), BF16),
        vmem((4, 256, D), BF16),
        vmem((TARGETS, D), BF16),
        vmem((TARGETS, D), BF16),
        vmem((MEMORY, 2 * FEATURES), BF16),
        vmem((MEMORY, 2 * FEATURES), BF16),
        vmem((TARGETS, FEATURES), F32),
        vmem((TARGETS, FEATURES), F32),
        vmem((TARGETS, FEATURES), BF16),
        vmem((TARGETS, FEATURES), BF16),
        vmem((TARGETS, FEATURES), BF16),
        vmem((TARGETS, FEATURES), BF16),
        vmem((TARGETS, MEMORY), F32),
        vmem((HEADS, TARGETS, MEMORY), BF16),
        vmem((HEADS, TARGETS, MEMORY), BF16),
        vmem((4, 128, D), BF16),
        vmem((3, OWN_ROWS, SIDE), BF16),
        vmem((2, OWN_ROWS // 2, SIDE), BF16),
        vmem((2, 4, OWN_ROWS, SIDE), BF16),
        vmem((3, OWN_ROWS, SIDE), BF16),
        vmem((3, OWN_ROWS, FEATURES), BF16),
        vmem((6, TARGETS, FEATURES), BF16),
        vmem((TARGETS, FEATURES), BF16),
        vmem((6, TARGETS, FEATURES), BF16),
        vmem((TARGETS, FEATURES), BF16),
        pltpu.SemaphoreType.DMA((N_SEMS,)),
        pltpu.SemaphoreType.DMA((N_SEMS,)),
        pltpu.SemaphoreType.DMA((N_LOCAL,)),
    ]
    results = pl.pallas_call(
        kernel,
        out_shape=(
            jax.ShapeDtypeStruct(tokens.shape, BF16),
            jax.ShapeDtypeStruct(cotangent.shape, BF16),
            jax.ShapeDtypeStruct(memory.shape, BF16),
        ),
        in_specs=[pl.BlockSpec(memory_space=pl.ANY)] * 7,
        out_specs=(pl.BlockSpec(memory_space=pltpu.VMEM),) * 3,
        scratch_shapes=scratch,
        compiler_params=pltpu.CompilerParams(
            collective_id=0, has_side_effects=True, vmem_limit_bytes=62 * 2**20
        ),
        cost_estimate=pl.CostEstimate(flops=23 * 10**9, bytes_accessed=18 * 2**20, transcendentals=2**19),
    )(tokens, cotangent, memory, w_query, w_key, w_value, w_out)
    return pl.pallas_call(
        hand_over,
        out_shape=tuple(jax.ShapeDtypeStruct(r.shape, r.dtype) for r in results),
        in_specs=[pl.BlockSpec(memory_space=pltpu.VMEM)] * 3,
        out_specs=(pl.BlockSpec(memory_space=pltpu.VMEM),) * 3,
    )(*results)


def solution(mesh):
    placed = (
        P("section", None, "tp"),
        P("section", None, "tp"),
        P("section", "tp"),
        P("section", None, "tp"),
        P("section", None, "tp"),
        P("section", None, "tp"),
        P("section", "tp", None),
    )
    return jax.shard_map(
        on_device,
        mesh=mesh,
        in_specs=placed,
        out_specs=(P("section", None, "tp"), P("section", None, "tp"), P("section", "tp")),
        check_vma=False,
    )
```

```python
import functools

import jax
import jax.numpy as jnp
from jax import lax
from jax.experimental import pallas as pl
from jax.experimental.pallas import tpu as pltpu
from jax.sharding import PartitionSpec as P

HEAD_SIZE = 256
HEADS = 2
FEATURES = 512
D = 4096
TARGETS = 256
MEMORY = 1024
OWN_ROWS = 64
SIDE = 2048
SCALE = HEAD_SIZE ** -0.5
BF16 = jnp.bfloat16
F32 = jnp.float32
N_SEMS = 128
N_LOCAL = 48


def dot(a, b):
    return lax.dot_general(a, b, (((1,), (0,)), ((), ())), preferred_element_type=F32)


def dot_nt(a, b):
    return lax.dot_general(a, b, (((1,), (1,)), ((), ())), preferred_element_type=F32)


def dot_tn(a, b):
    return lax.dot_general(a, b, (((0,), (0,)), ((), ())), preferred_element_type=F32)


def aligned(start, size):
    return pl.ds(pl.multiple_of(start, size), size)


def add_rows(dst, srcs):
    rows = dst.shape[0]

    def step(i, _):
        part = aligned(i * 16, 16)
        total = srcs[0][part, :].astype(F32)
        for src in srcs[1:]:
            total = total + src[part, :].astype(F32)
        dst[part, :] = total.astype(dst.dtype)
        return 0

    lax.fori_loop(0, rows // 16, step, 0)


def kernel(
    tokens, cotangent, memory, w_query, w_key, w_value, w_out,
    attended, grad_tokens, grad_memory,
    wkv, wq, wo, mem, tok, cot, kv, gkv, queries_acc, gctx_acc, queries, gctx, ctx, gq, probs, probs_b, dscores,
    core_in, opposite_in, relay_in, final_in, z_in, y_in, att_in, att_z, tgt_in, tgt_z,
    send_sem, recv_sem, local_sem,
):
    section = lax.axis_index("section")
    tp = lax.axis_index("tp")
    c = lax.rem(section, 2)
    x = lax.rem(section // 2, 4)
    y = tp // 2
    zh = lax.rem(tp, 2)
    z = zh * 2 + section // 8

    def device(dx=0, dy=0, dz=0, dc=0):
        to_x, to_y, to_z = lax.rem(x + dx, 4), lax.rem(y + dy, 4), lax.rem(z + dz, 4)
        to_c = lax.rem(c + dc, 2)
        return ((lax.rem(to_z, 2) * 4 + to_x) * 2 + to_c, to_y * 2 + to_z // 2)

    counter = [0, 0]
    sends = []

    def remote(src, dst, where):
        i = counter[0]
        counter[0] += 1
        copy = pltpu.make_async_remote_copy(
            src_ref=src, dst_ref=dst, send_sem=send_sem.at[i], recv_sem=recv_sem.at[i],
            device_id=device(**where), device_id_type=pl.DeviceIdType.MESH,
        )
        copy.start()
        sends.append(copy)
        return copy

    def local(src, dst):
        i = counter[1]
        counter[1] += 1
        copy = pltpu.make_async_copy(src, dst, local_sem.at[i])
        copy.start()
        return copy

    def flush():
        for copy in sends:
            copy.wait_send()
        sends.clear()

    XP, XM, YP, YM = dict(dx=1), dict(dx=3), dict(dy=1), dict(dy=3)
    CORE, ZFAR = dict(dc=1), dict(dz=2)

    def x_at(dx):
        return lax.rem(x + dx, 4)

    def side(high):
        return aligned(high * SIDE, SIDE)

    def piece(dx, core, dz, half=None):
        to_z = lax.rem(z + dz, 4)
        row = core * 128 + lax.rem(to_z, 2) * 64
        rows = aligned(row, 64) if half is None else aligned(row + half * 32, 32)
        return mem.at[x_at(dx), rows, side(to_z // 2)]

    def block(buf, high, dy):
        return buf.at[:, aligned(high * SIDE + lax.rem(y + dy, 4) * FEATURES, FEATURES)]

    own_mem = mem.at[x, aligned(c * 128 + lax.rem(z, 2) * 64, 64), aligned(zh * SIDE + y * FEATURES, FEATURES)]
    near, far = zh, 1 - zh

    mem_load = local(memory, own_mem)
    tok_load = local(tokens.at[0], block(tok, near, 0))
    cot_load = local(cotangent.at[0], block(cot, near, 0))
    barrier = pltpu.get_barrier_semaphore()
    peers = [XP, XM, YP, YM, dict(dy=2), dict(dz=1), dict(dz=3), ZFAR, CORE]
    for where in peers:
        pl.semaphore_signal(barrier, inc=1, device_id=device(**where), device_id_type=pl.DeviceIdType.MESH)
    pl.semaphore_wait(barrier, len(peers))

    mem_y = {dy: remote(memory, own_mem, dict(dy=dy)) for dy in (1, 3, 2)}
    right, left, core_own, mem_z = {}, {}, {}, {}
    def spread_targets():
        t, g = tokens.at[0], cotangent.at[0]
        t_dst, g_dst = block(tok, near, 0), block(cot, near, 0)
        t_right = remote(t, t_dst, YP)
        g_left = remote(g, g_dst, YM)
        g_right = remote(g, g_dst, YP)
        t_left = remote(t, t_dst, YM)
        return t_right, g_left, g_right, t_left

    right[0] = [remote(memory, own_mem, XP)]
    left[0] = [remote(memory, own_mem, XM)]
    mem_z[1] = [remote(memory, own_mem, dict(dz=1))]
    mem_z[3] = [remote(memory, own_mem, dict(dz=3))]
    tok_z = remote(tokens.at[0], block(tok, near, 0), ZFAR)
    near_ring = spread_targets()
    mem_load.wait()
    for dy in (1, 3, 2):
        mem_y[dy].wait_recv()
        here = mem.at[
            x, aligned(c * 128 + lax.rem(z, 2) * 64, 64), aligned(zh * SIDE + lax.rem(y + 4 - dy, 4) * FEATURES, FEATURES)
        ]
        right[0].append(remote(here, here, XP))
        left[0].append(remote(here, here, XM))
        mem_z[1].append(remote(here, here, dict(dz=1)))
        mem_z[3].append(remote(here, here, dict(dz=3)))
    own = piece(0, c, 0)
    core_right, core_left, core_opposite = {}, {}, {}
    on_right, on_left = {}, {}

    def spread(dz):
        here = piece(0, c, dz)
        right[dz] = [remote(here, here, XP)]
        left[dz] = [remote(here, here, XM)]
        core_own[dz] = remote(here, here, CORE)

    def spread_far(buf):
        here = block(buf, far, 0)
        return remote(here, here, YP), remote(here, here, YM)

    def arrive_x(dz):
        for copy in right[dz]:
            copy.wait_recv()
        if dz in (0, 2):
            on_right[dz] = remote(piece(3, c, dz, 0), piece(3, c, dz, 0), XP)
        core_left[dz] = remote(piece(3, c, dz), piece(3, c, dz), CORE)
        for copy in left[dz]:
            copy.wait_recv()
        if dz in (0, 2):
            on_left[dz] = remote(piece(1, c, dz, 1), piece(1, c, dz, 1), XM)
        core_right[dz] = remote(piece(1, c, dz), piece(1, c, dz), CORE)

    def arrive_opposite(dz):
        on_right[dz].wait_recv()
        a = remote(piece(2, c, dz, 0), piece(2, c, dz, 0), CORE)
        on_left[dz].wait_recv()
        b = remote(piece(2, c, dz, 1), piece(2, c, dz, 1), CORE)
        core_opposite[dz] = (a, b)

    def arrive_opposite_z(dz):
        opposite_z[4 - dz].wait_recv()
        core_opposite[dz] = (remote(piece(2, c, dz), piece(2, c, dz), CORE),)

    def forward_targets(high, ring):
        t_right, g_left, g_right, t_left = ring
        t_right.wait_recv()
        t_on = remote(block(tok, high, 3), block(tok, high, 3), YP)
        g_left.wait_recv()
        g_on = remote(block(cot, high, 1), block(cot, high, 1), YM)
        return t_on, g_on

    def keys_values(dx, chunks=(0, 2)):
        to_x = x_at(dx)
        rows = aligned(to_x * 256, 256)

        def step(n, _):
            cols = aligned(n * 512, 512)
            kv[rows, cols] = dot(mem[to_x], wkv[:, cols]).astype(BF16)
            return 0

        lax.fori_loop(chunks[0], chunks[1], step, 0)

    core_own[0] = remote(own, own, CORE)
    kv_loads, q_loads, o_loads = [], [], []
    for high in range(2):
        for row in range(4):
            src = pl.ds((row * 2 + high) * FEATURES, FEATURES)
            dst = pl.ds(high * SIDE + row * FEATURES, FEATURES)
            kv_loads.append(local(w_key.at[0, src, :], wkv.at[dst, pl.ds(0, FEATURES)]))
            kv_loads.append(local(w_value.at[0, src, :], wkv.at[dst, pl.ds(FEATURES, FEATURES)]))
    tok_z.wait_recv()
    far_tok = spread_far(tok)
    arrive_x(0)
    for dz in (1, 3):
        for copy in mem_z[4 - dz]:
            copy.wait_recv()
        spread(dz)
    mem_z[2] = remote(own, own, ZFAR)
    cot_z = remote(cotangent.at[0], block(cot, near, 0), ZFAR)
    for high in range(2):
        for row in range(4):
            src = pl.ds((row * 2 + high) * FEATURES, FEATURES)
            dst = pl.ds(high * SIDE + row * FEATURES, FEATURES)
            q_loads.append(local(w_query.at[0, src, :], wq.at[dst, :]))
            o_loads.append(local(w_out.at[0, :, src], wo.at[:, dst]))

    near_on = forward_targets(near, near_ring)
    arrive_opposite(0)
    opposite_z = {dz: remote(piece(2, c, 0), piece(2, c, 0), dict(dz=dz)) for dz in (1, 3)}
    mem_z[2].wait_recv()
    spread(2)
    cot_z.wait_recv()
    far_cot = spread_far(cot)
    for copy in kv_loads:
        copy.wait()
    for dz in (0, 1, 3, 2):
        core_own[dz].wait_recv()
    keys_values(0)
    arrive_x(1)
    arrive_x(3)
    far_tok[0].wait_recv()
    far_t_on = remote(block(tok, far, 3), block(tok, far, 3), YP)

    def complete(ring, on):
        t_right, g_left, g_right, t_left = ring
        g_right.wait_recv()
        t_left.wait_recv()
        on[0].wait_recv()
        on[1].wait_recv()

    complete(near_ring, near_on)
    tok_load.wait()
    cot_load.wait()
    for copy in q_loads:
        copy.wait()
    for copy in o_loads:
        copy.wait()

    def project_near():
        queries_acc[...] = dot(tok[:, side(near)], wq[side(near), :])
        gctx_acc[...] = dot_nt(cot[:, side(near)], wo[:, side(near)])

    project_near()
    arrive_opposite_z(1)
    arrive_opposite_z(3)
    arrive_x(2)
    far_cot[1].wait_recv()
    far_g_on = remote(block(cot, far, 1), block(cot, far, 1), YM)
    far_on = (far_t_on, far_g_on)
    far_ring = (far_tok[0], far_cot[1], far_cot[0], far_tok[1])
    for dz in (0, 1, 3, 2):
        core_right[dz].wait_recv()
    keys_values(1)
    for dz in (0, 1, 3, 2):
        core_left[dz].wait_recv()
    keys_values(3, (0, 1))
    arrive_opposite(2)
    keys_values(3, (1, 2))
    for dz in (0, 1, 3, 2):
        for copy in core_opposite[dz]:
            copy.wait_recv()
    keys_values(2)
    complete(far_ring, far_on)

    def project_far():
        queries[...] = (queries_acc[...] + dot(tok[:, side(far)], wq[side(far), :])).astype(BF16)
        gctx[...] = (gctx_acc[...] + dot_nt(cot[:, side(far)], wo[:, side(far)])).astype(BF16)

    project_far()
    flush()

    for h in range(HEADS):
        k_cols = pl.ds(h * HEAD_SIZE, HEAD_SIZE)
        v_cols = pl.ds(FEATURES + h * HEAD_SIZE, HEAD_SIZE)
        scores = dot_nt(queries[:, k_cols], kv[:, k_cols]) * SCALE
        top = jnp.max(scores, axis=-1, keepdims=True)
        weights = jnp.exp(scores - top)
        p = weights / jnp.sum(weights, axis=-1, keepdims=True)
        probs[...] = p
        p_b = p.astype(BF16)
        probs_b[h] = p_b
        grad_probs = dot_nt(gctx[:, k_cols], kv[:, v_cols])
        p = probs[...]
        delta = jnp.sum(grad_probs * p, axis=-1, keepdims=True)
        ds = (p * (grad_probs - delta) * SCALE).astype(BF16)
        dscores[h] = ds
        gkv[:, k_cols] = dot_tn(ds, queries[:, k_cols]).astype(BF16)
        gkv[:, v_cols] = dot_tn(probs_b[h], gctx[:, k_cols]).astype(BF16)

    def memory_terms(dx, high):
        to_x = x_at(dx)
        rows = aligned(to_x * 256, 256)

        def step(n, _):
            cols = aligned(high * SIDE + n * 512, 512)
            mem[to_x, :, cols] = dot_nt(gkv[rows, :], wkv[cols, :]).astype(BF16)
            return 0

        lax.fori_loop(0, 4, step, 0)
        return remote(
            mem.at[to_x, aligned((1 - c) * 128, 128), side(high)], core_in.at[to_x, :, side(high)], CORE
        )

    zl = lax.rem(z, 2)

    def part(dx, high, low):
        return mem.at[x_at(dx), aligned(c * 128 + low * 64, 64), side(high)]

    def pair_sum(dx, high, low, extra=()):
        here = part(dx, high, low)
        other = core_in.at[x_at(dx), aligned(low * 64, 64), side(high)]
        add_rows(here, [here, other] + list(extra))
        return here

    def far_relay(buf, inbox):
        return remote(block(buf, far, 2), inbox.at[0], YP)

    def near_relay(buf, inbox):
        return remote(block(buf, near, 2), inbox.at[1], YM)

    def far_on_left(buf, inbox, terms):
        terms(far, 3)
        return remote(block(buf, far, 3), inbox.at[3], YM)

    def near_on_right(buf, inbox, terms):
        terms(near, 1)
        return remote(block(buf, near, 1), inbox.at[2], YP)

    def far_on_right(buf, inbox, a_relay):
        a_relay.wait_recv()
        here = block(buf, far, 1)
        add_rows(here, [here, inbox.at[0]])
        return remote(here, inbox.at[4], YP)

    def near_on_left(buf, inbox, b_relay):
        b_relay.wait_recv()
        here = block(buf, near, 3)
        add_rows(here, [here, inbox.at[1]])
        return remote(here, inbox.at[5], YM)

    def ring_far(buf, inbox, z_box, a_left, a_right):
        a_left.wait_recv()
        a_right.wait_recv()
        here = block(buf, far, 0)
        add_rows(here, [here, inbox.at[3], inbox.at[4]])
        return remote(here, z_box, ZFAR)

    def ring_near(buf, inbox, z_box, b_right, b_left, z_copy, out):
        b_right.wait_recv()
        b_left.wait_recv()
        z_copy.wait_recv()
        add_rows(out.at[0], [block(buf, near, 0), inbox.at[2], inbox.at[5], z_box])

    def out_terms(high, dy):
        cols = aligned(high * SIDE + lax.rem(y + dy, 4) * FEATURES, FEATURES)
        tok[:, cols] = dot(ctx[...], wo[:, cols]).astype(BF16)

    def target_terms(high, dy):
        rows = aligned(high * SIDE + lax.rem(y + dy, 4) * FEATURES, FEATURES)
        cot[:, rows] = dot_nt(gq[...], wq[rows, :]).astype(BF16)

    lows = (zl, 1 - zl)
    far_lows, near_lows = lows, lows[::-1]

    def x_final_far(i):
        far_left[i].wait_recv()
        far_right[i].wait_recv()
        here = pair_sum(0, far, far_lows[i], [final_in.at[0, i], final_in.at[1, i]])
        if i == 0:
            return remote(here, z_in.at[0], ZFAR)
        return remote(here, z_in.at[1], dict(dz=3 - 2 * zl))

    def x_final_near(i):
        near_right[i].wait_recv()
        near_left[i].wait_recv()
        here = pair_sum(0, near, near_lows[i], [final_in.at[0, 2 + i], final_in.at[1, 2 + i]])
        if i == 0:
            return remote(here, z_in.at[2], dict(dz=1 + 2 * zl))
        return here

    core_2f = memory_terms(2, far)
    core_3f = memory_terms(3, far)
    for h in range(HEADS):
        cols = pl.ds(h * HEAD_SIZE, HEAD_SIZE)
        v_cols = pl.ds(FEATURES + h * HEAD_SIZE, HEAD_SIZE)
        ctx[:, cols] = dot(probs_b[h], kv[:, v_cols]).astype(BF16)
    out_terms(far, 2)
    att_far_relay = far_relay(tok, att_in)
    att_far_left = far_on_left(tok, att_in, out_terms)
    core_2f.wait_recv()
    opposite_far = remote(pair_sum(2, far, 1 - zl), opposite_in.at[1], dict(dz=3 - 2 * zl))
    relay_right = remote(pair_sum(2, far, zl), relay_in.at[0], XP)
    core_2n = memory_terms(2, near)
    core_3f.wait_recv()
    far_left = [remote(pair_sum(3, far, zl), final_in.at[1, 0], XM)]
    for h in range(HEADS):
        cols = pl.ds(h * HEAD_SIZE, HEAD_SIZE)
        gq[:, cols] = dot(dscores[h], kv[:, cols]).astype(BF16)
    out_terms(far, 1)
    target_terms(far, 2)
    core_1f = memory_terms(1, far)
    core_2n.wait_recv()
    opposite_near = remote(pair_sum(2, near, 1 - zl), opposite_in.at[0], dict(dz=1 + 2 * zl))
    target_terms(far, 1)
    far_left.append(remote(pair_sum(3, far, 1 - zl), final_in.at[1, 1], XM))
    core_1n = memory_terms(1, near)
    out_terms(near, 2)
    att_far_right = far_on_right(tok, att_in, att_far_relay)
    tgt_far_relay = far_relay(cot, tgt_in)
    tgt_far_left = far_on_left(cot, tgt_in, target_terms)
    core_1f.wait_recv()
    relay_right.wait_recv()
    far_right = [remote(pair_sum(1, far, zl, [relay_in.at[0]]), final_in.at[0, 0], XP)]
    opposite_near.wait_recv()
    opposite_far.wait_recv()
    relay_left = remote(
        pair_sum(2, near, zl, [opposite_in.at[0], opposite_in.at[1]]), relay_in.at[1], XM
    )
    att_near_relay = near_relay(tok, att_in)
    core_0f = memory_terms(0, far)
    far_right.append(remote(pair_sum(1, far, 1 - zl), final_in.at[0, 1], XP))
    out_terms(far, 0)
    core_3n = memory_terms(3, near)
    target_terms(near, 2)
    core_0f.wait_recv()
    att_far = ring_far(tok, att_in, att_z, att_far_left, att_far_right)
    z_far0 = x_final_far(0)
    core_1n.wait_recv()
    near_right = [remote(pair_sum(1, near, 1 - zl), final_in.at[0, 2], XP)]
    core_3n.wait_recv()
    near_left = [remote(pair_sum(3, near, 1 - zl), final_in.at[1, 2], XM)]
    tgt_near_relay = near_relay(cot, tgt_in)
    att_near_right = near_on_right(tok, att_in, out_terms)
    target_terms(far, 0)
    out_terms(near, 3)
    target_terms(near, 3)
    tgt_far_right = far_on_right(cot, tgt_in, tgt_far_relay)
    z_far1 = x_final_far(1)
    near_right.append(remote(pair_sum(1, near, zl), final_in.at[0, 3], XP))
    relay_left.wait_recv()
    near_left.append(remote(pair_sum(3, near, zl, [relay_in.at[1]]), final_in.at[1, 3], XM))
    tgt_near_right = near_on_right(cot, tgt_in, target_terms)
    att_near_left = near_on_left(tok, att_in, att_near_relay)
    core_0n = memory_terms(0, near)
    out_terms(near, 0)
    target_terms(near, 0)
    core_0n.wait_recv()
    tgt_near_left = near_on_left(cot, tgt_in, tgt_near_relay)
    z_near0 = x_final_near(0)
    tgt_far = ring_far(cot, tgt_in, tgt_z, tgt_far_left, tgt_far_right)
    here = x_final_near(1)
    for copy in (z_far0, z_near0, z_far1):
        copy.wait_recv()
    add_rows(here, [here, z_in.at[0], z_in.at[1], z_in.at[2]])

    def y_part(dy):
        return mem.at[
            x, aligned(c * 128 + zl * 64, 64), aligned(zh * SIDE + lax.rem(y + dy, 4) * FEATURES, FEATURES)
        ]

    y_copies = [remote(y_part(dy), y_in.at[dy - 1], dict(dy=dy)) for dy in (2, 1, 3)]
    ring_near(tok, att_in, att_z, att_near_right, att_near_left, att_far, attended)
    ring_near(cot, tgt_in, tgt_z, tgt_near_right, tgt_near_left, tgt_far, grad_tokens)
    for copy in y_copies:
        copy.wait_recv()
    add_rows(grad_memory, [y_part(0), y_in.at[0], y_in.at[1], y_in.at[2]])
    flush()


def hand_over(a_in, b_in, c_in, a_out, b_out, c_out):
    a_out[...] = a_in[...]
    b_out[...] = b_in[...]
    c_out[...] = c_in[...]


def on_device(tokens, cotangent, memory, w_query, w_key, w_value, w_out):
    vmem = pltpu.VMEM
    scratch = [
        vmem((D, 2 * FEATURES), BF16),
        vmem((D, FEATURES), BF16),
        vmem((FEATURES, D), BF16),
        vmem((4, 256, D), BF16),
        vmem((TARGETS, D), BF16),
        vmem((TARGETS, D), BF16),
        vmem((MEMORY, 2 * FEATURES), BF16),
        vmem((MEMORY, 2 * FEATURES), BF16),
        vmem((TARGETS, FEATURES), F32),
        vmem((TARGETS, FEATURES), F32),
        vmem((TARGETS, FEATURES), BF16),
        vmem((TARGETS, FEATURES), BF16),
        vmem((TARGETS, FEATURES), BF16),
        vmem((TARGETS, FEATURES), BF16),
        vmem((TARGETS, MEMORY), F32),
        vmem((HEADS, TARGETS, MEMORY), BF16),
        vmem((HEADS, TARGETS, MEMORY), BF16),
        vmem((4, 128, D), BF16),
        vmem((2, OWN_ROWS, SIDE), BF16),
        vmem((2, OWN_ROWS, SIDE), BF16),
        vmem((2, 4, OWN_ROWS, SIDE), BF16),
        vmem((3, OWN_ROWS, SIDE), BF16),
        vmem((3, OWN_ROWS, FEATURES), BF16),
        vmem((6, TARGETS, FEATURES), BF16),
        vmem((TARGETS, FEATURES), BF16),
        vmem((6, TARGETS, FEATURES), BF16),
        vmem((TARGETS, FEATURES), BF16),
        pltpu.SemaphoreType.DMA((N_SEMS,)),
        pltpu.SemaphoreType.DMA((N_SEMS,)),
        pltpu.SemaphoreType.DMA((N_LOCAL,)),
    ]
    results = pl.pallas_call(
        kernel,
        out_shape=(
            jax.ShapeDtypeStruct(tokens.shape, BF16),
            jax.ShapeDtypeStruct(cotangent.shape, BF16),
            jax.ShapeDtypeStruct(memory.shape, BF16),
        ),
        in_specs=[pl.BlockSpec(memory_space=pl.ANY)] * 7,
        out_specs=(pl.BlockSpec(memory_space=pltpu.VMEM),) * 3,
        scratch_shapes=scratch,
        compiler_params=pltpu.CompilerParams(
            collective_id=0, has_side_effects=True, vmem_limit_bytes=62 * 2**20
        ),
        cost_estimate=pl.CostEstimate(flops=23 * 10**9, bytes_accessed=18 * 2**20, transcendentals=2**19),
    )(tokens, cotangent, memory, w_query, w_key, w_value, w_out)
    return pl.pallas_call(
        hand_over,
        out_shape=tuple(jax.ShapeDtypeStruct(r.shape, r.dtype) for r in results),
        in_specs=[pl.BlockSpec(memory_space=pltpu.VMEM)] * 3,
        out_specs=(pl.BlockSpec(memory_space=pltpu.VMEM),) * 3,
    )(*results)


def solution(mesh):
    placed = (
        P("section", None, "tp"),
        P("section", None, "tp"),
        P("section", "tp"),
        P("section", None, "tp"),
        P("section", None, "tp"),
        P("section", None, "tp"),
        P("section", "tp", None),
    )
    return jax.shard_map(
        on_device,
        mesh=mesh,
        in_specs=placed,
        out_specs=(P("section", None, "tp"), P("section", None, "tp"), P("section", "tp")),
        check_vma=False,
    )
```
